128 devices in a mesh: section: 4 (over x_lo, core), tp: 8 (over y, x_hi), src: 4 (over z).
Axes of the slice: x: 4 (x_hi: 2, x_lo: 2; x = x_hi * 2 + x_lo), y: 4, z: 4, core: 2. Of those that a mesh axis runs over, the one named last changes fastest.
Arguments:
- prefill_pool: bfloat16 [4, 4, 8, 16, 4, 8, 16, 256], P('src', 'section', 'tp'), may hold values from -6 to 6
- block_scales: bfloat16 [4, 4, 8, 16, 4, 8, 2], P('src', 'section', 'tp'), may hold values from 0.25 to 2
- block_table: int32 [4, 4, 8, 16], P('src', 'section', 'tp'), may hold values from 0 to 15, each once within a row
- prompt_len: int32 [4, 4], replicated, may hold values from 1 to 2048, 5120 in all within a row
- dest_group: int32 [4, 4, 1], replicated, may hold values from 0 to 3; in each aligned block of 4 rows (0 to 3, 4 to 7, ..., all dimensions but the last counted through in order) at most 2 rows name the same one
- res_len: int32 [4, 8], P('src'), may hold values from 1 to 3072, 13824 in all within a row
- res_cache: bfloat16 [4, 32, 8, 3072, 256], P('section', 'src', 'tp'), may hold values from -6 to 6
- queries: bfloat16 [4, 64, 8, 8, 2048], P('section', 'src', 'tp'), may hold values from -1000 to 1000
- new_kv: bfloat16 [4, 64, 8, 8, 256], P('section', 'src', 'tp'), may hold values from -6 to 6
Outputs:
- attn_out: bfloat16 [4, 64, 8, 8, 2048], P('section', 'src', 'tp')
- arrived_cache: bfloat16 [4, 32, 8, 2048, 256], P('section', 'src', 'tp')
The draws below stay inside these ranges and needn't reach their ends.
Inputs may be any that keep to these rules, and one draw needn't show every extreme that they name: `dest_group`: at most 2 requests of one prefill group name the same decode group, and in some group exactly 2 do. `block_table`: each prefill device's row is a permutation of its 16 pool blocks. `prompt_len`: each prefill group's lengths sum to (4 + 1) * 1024 and the longest is exactly 2048. `res_len`: each decode group's lengths sum to (8 + 1) * 1536 and the longest is exactly 3072.
All inputs are finite; a program needn't handle non-finite values.
Results may differ from the reference program's by a relative error of at most 0.0066.
Values may be sent and summed in bfloat16 or wider, within the bound.
No kernel may reach another device: no remote copies, remote signals or barrier semaphores. Data moves between devices by JAX's collectives and lax.ppermute only.
A program may use at most 192 MiB of HBM per device.

```python
import math
import jax
import jax.numpy as jnp
import numpy as np
from jax import lax

KVH = 8
HD = 128
QPK = 16
NEW = 8
BLK = 16
PROMPT = 2048
RP = 4
RES = 8
CTX = 3072
LAYERS = 4
CAPR = 2
SLOTS = 8
ROWS = 16
NB = 128
PB = 16
N_SECTION = 4
N_TP = 8
N_SRC = 4


def fresh_pieces(key):
    query_key, pair_key = jax.random.split(key)
    query_shape = (LAYERS, N_SRC * ROWS, KVH, NEW, QPK * HD)
    pair_shape = (LAYERS, N_SRC * ROWS, KVH, NEW, 2 * HD)
    base_query = jax.random.truncated_normal(query_key, -6.0, 6.0, query_shape, jnp.float32)
    fresh_pairs = jax.random.truncated_normal(pair_key, -6.0, 6.0, pair_shape, jnp.float32)
    return (base_query, fresh_pairs)


def draw_new_kv(key, part):
    base_query, fresh_pairs = fresh_pieces(key)
    return fresh_pairs.astype(jnp.bfloat16)


def draw_queries(key, part):
    base_query, fresh_pairs = fresh_pieces(key)
    return base_query.astype(jnp.bfloat16)


def block_levels(rng, dims, cuts, low, high):
    def one(dim, blocks):
        draws = jax.random.uniform(jax.random.fold_in(jax.random.fold_in(rng, 6), dim), (blocks,), jnp.float32, low / len(cuts), high / len(cuts))
        return jnp.repeat(jnp.exp(draws), dims[dim] // blocks).reshape((-1,) + (1,) * (len(dims) - dim - 1))

    level = one(*cuts[0])
    for cut in cuts[1:]:
        level = level * one(*cut)
    return level


def split_up(amount, total, most, lean):
    weights = [(1 << 20) // math.isqrt(standing ** lean) + 1 for standing in range(2, amount + 1)]
    rest, given = total - most - (amount - 1), [1] * (amount - 1)
    while rest > 0:
        free = [i for i in range(amount - 1) if given[i] < most]
        whole, budget = sum([weights[i] for i in free]), rest
        for i in free:
            more = min(most - given[i], max(1, budget * weights[i] // whole), rest)
            given[i] = given[i] + more
            rest = rest - more
    return np.array([most] + given)


def ragged_sizes(rng, amount, total, limit, lean):
    if amount == 2:
        one = jax.random.randint(rng, (), max(1, total - limit), min(limit, total - 1) + 1)
        return jnp.stack([one, total - one])
    sizes = jnp.asarray(split_up(amount, total, limit, lean), jnp.int32)
    pairs = (amount - 1) // 2
    donor, taker = sizes[1:1 + 2 * pairs:2], sizes[2:2 + 2 * pairs:2]
    slack = jnp.minimum(donor - 1, limit - taker)
    passed = jax.random.randint(jax.random.fold_in(rng, 1), (pairs,), 0, 1 << 20) % (slack + 1)
    sizes = sizes.at[1:1 + 2 * pairs:2].set(donor - passed).at[2:2 + 2 * pairs:2].set(taker + passed)
    return sizes[jax.random.permutation(jax.random.fold_in(rng, 2), amount)]


def assign_block(rng, own, number, rows, amount, top, most, slope):
    ranking = jax.random.permutation(rng, amount)
    packed, ordinary = shares(amount, rows * top, most, slope, True), shares(amount, rows * top, most, slope, False)
    places = jnp.arange(amount)

    def named(sizes, rotation):
        used = int((sizes > 0).sum())
        fixed = max(1, used // 4)
        shifted = fixed + (places - fixed + rotation * (used - fixed)) % max(1, amount - fixed)
        return jnp.zeros((amount,), jnp.int32).at[ranking[jnp.where(places < fixed, places, shifted)]].set(jnp.asarray(sizes, jnp.int32))

    sizes = jnp.where(number % 4 == 0, named(packed, number // 4), named(ordinary, number - number // 4 - 1))
    mixed = jax.random.permutation(jax.random.fold_in(own, 3), amount)
    donor, sink = mixed[0:amount // 2 * 2:2], mixed[1:amount // 2 * 2:2]
    room = jnp.minimum(sizes[donor] - 1, most - sizes[sink]) // 2
    room = jnp.where((donor == ranking[0]) | (sink == ranking[0]) | (sizes[sink] == 0), 0, jnp.maximum(room, 0))
    shifted = jax.random.randint(jax.random.fold_in(own, 4), (amount // 2,), 0, 1 << 20) % (room + 1)
    sizes = sizes.at[donor].add(-shifted).at[sink].add(shifted)
    items = jnp.searchsorted(jnp.cumsum(sizes), jnp.arange(rows * top), side="right").astype(jnp.int32)
    grid = items.reshape(top, rows).T
    grid = grid[jax.random.permutation(jax.random.fold_in(own, 1), rows)]
    rotation = jax.random.randint(jax.random.fold_in(own, 2), (rows, 1), 0, top)
    return jnp.take_along_axis(grid, (jnp.arange(top)[None, :] + rotation) % top, axis=1)


def shares(amount, total, limit, slope, full):
    portions = [(1 << 20) // math.isqrt(grade ** slope) + 1 for grade in range(1, amount + 1)]
    largest = limit if full else min(limit, max(-(-total // amount), total * portions[0] // sum(portions)))
    least = 1 if total - largest >= amount - 1 else 0
    given, spare = [largest] + [least] * (amount - 1), total - largest - least * (amount - 1)
    while spare > 0:
        candidates = [i for i in range(1, amount) if given[i] < largest] or [i for i in range(1, amount) if given[i] < limit]
        mass, remaining = sum([portions[i] for i in candidates]), spare
        for i in candidates:
            extra = min(limit - given[i], max(1, remaining * portions[i] // mass), spare)
            given[i] = given[i] + extra
            spare = spare - extra
    return np.array(given)


def centred(stream_key, shape, width, most, cuts=(), held_as=jnp.bfloat16):
    entries = width * jax.random.normal(stream_key, shape, jnp.float32)
    if cuts:
        entries = entries * block_levels(stream_key, shape, cuts, -0.22, 0.18)
    return jnp.clip(entries, -most, most).astype(held_as)


def setup_inputs(seed: int = 0) -> dict:
    keys = jax.random.split(jax.random.key(seed), 10)
    prefill_pool = centred(keys[0], (N_SRC, N_SECTION, N_TP, PB, LAYERS, KVH, BLK, 2 * HD), 1.0, 6.0, ((0, 4), (1, 4), (2, 8)))
    block_scales = jnp.clip(jnp.exp(math.log(2.0) - 2.0794415 * jax.random.uniform(keys[1], (N_SRC, N_SECTION, N_TP, PB, LAYERS, KVH, 2), jnp.float32) ** block_levels(keys[1], (N_SRC, N_SECTION, N_TP, PB, LAYERS, KVH, 2), ((0, 4), (1, 4), (2, 8)), -0.2, 0.2)), 0.25, 2.0).astype(jnp.bfloat16)
    block_table = jax.vmap(lambda own: jax.random.permutation(own, PB))(jax.random.split(keys[2], N_SRC * N_SECTION * N_TP)).reshape((N_SRC, N_SECTION, N_TP, PB)).astype(jnp.int32)
    prompt_len = jax.vmap(lambda own: ragged_sizes(own, RP, (RP + 1) * PROMPT // 2, PROMPT, 1))(jax.random.split(keys[3], N_SRC)).reshape((N_SRC, RP)).astype(jnp.int32)
    dest_group_keys = jax.random.split(jax.random.fold_in(keys[4], 1), N_SRC * RP // RP)
    dest_group_turns = jax.random.permutation(jax.random.fold_in(keys[4], 3), N_SRC * RP // RP)
    dest_group = jax.vmap(lambda own, number: assign_block(jax.random.fold_in(keys[4], 2), own, number, RP, N_SRC, 1, CAPR, 1))(dest_group_keys, dest_group_turns).reshape((N_SRC, RP, 1))
    res_len = jax.vmap(lambda own: ragged_sizes(own, RES, (RES + 1) * CTX // 2, CTX, 1))(jax.random.split(keys[5], N_SRC)).reshape((N_SRC, RES)).astype(jnp.int32)
    res_cache = centred(keys[6], (LAYERS, N_SRC * RES, KVH, CTX, 2 * HD), 1.0, 6.0, ((0, 4), (1, 4), (2, 8)))
    queries = draw_queries(jax.random.fold_in(keys[9], 71), 0)
    new_kv = draw_new_kv(jax.random.fold_in(keys[9], 71), 0)
    return dict(prefill_pool=prefill_pool, block_scales=block_scales, block_table=block_table, prompt_len=prompt_len, dest_group=dest_group, res_len=res_len, res_cache=res_cache, queries=queries, new_kv=new_kv)


def attend(query_rows, context, length, fresh_kv):
    row_count, head_count, step_count, full_width = query_rows.shape
    head_dim = context.shape[-1] // 2
    group_size = full_width // head_dim
    flattened = query_rows.reshape(row_count, head_count, step_count * group_size, head_dim).astype(jnp.float32)
    score_scale = head_dim ** -0.5
    history = jnp.einsum("rhmd,rhtd->rhmt", flattened, context[..., :head_dim].astype(jnp.float32)) * score_scale
    places = jnp.arange(context.shape[2])
    history = jnp.where(places[None, None, None, :] < length[:, None, None, None], history, -jnp.inf)
    own_scores = jnp.einsum("rhmd,rhpd->rhmp", flattened, fresh_kv[..., :head_dim].astype(jnp.float32)) * score_scale
    position = jnp.arange(step_count * group_size) // group_size
    own_scores = jnp.where(jnp.arange(step_count)[None, :] <= position[:, None], own_scores, -jnp.inf)
    highest = jnp.maximum(jnp.max(history, axis=-1), jnp.max(own_scores, axis=-1))[..., None]
    history_w = jnp.exp(history - highest)
    own_w = jnp.exp(own_scores - highest)
    denominator = jnp.sum(history_w, axis=-1, keepdims=True) + jnp.sum(own_w, axis=-1, keepdims=True)
    history_w = (history_w / denominator).astype(jnp.bfloat16)
    own_w = (own_w / denominator).astype(jnp.bfloat16)
    blended = jnp.einsum("rhmt,rhtd->rhmd", history_w.astype(jnp.float32), context[..., head_dim:].astype(jnp.float32))
    blended = blended + jnp.einsum("rhmp,rhpd->rhmd", own_w.astype(jnp.float32), fresh_kv[..., head_dim:].astype(jnp.float32))
    return blended.reshape(row_count, head_count, step_count, full_width).astype(jnp.bfloat16)


def one_row(items):
    query_rows, context, length, fresh_kv = items
    return attend(query_rows[None], context[None], length[None], fresh_kv[None])[0]


def take_rows(table_rows, pool_rows):
    return jnp.take(pool_rows, table_rows, axis=0)


def reference(prefill_pool, block_scales, block_table, prompt_len, dest_group, res_len, res_cache, queries, new_kv):
    group_count, section_count, rank_count, pool_blocks = block_table.shape
    requests = prompt_len.shape[1]
    per_rank = pool_blocks // requests
    layers, kv_heads, block_len, row_width = prefill_pool.shape[4:]
    head_dim = row_width // 2
    slices = section_count * rank_count
    gather_all = jax.vmap(jax.vmap(jax.vmap(take_rows)))
    codes = gather_all(block_table, prefill_pool)
    codes = codes.reshape(group_count, slices, requests, per_rank, layers, kv_heads, block_len, row_width)
    codes = codes.transpose(0, 2, 4, 5, 1, 3, 6, 7).reshape(group_count * requests, layers, kv_heads, PROMPT, row_width)
    factors = gather_all(block_table, block_scales)
    factors = factors.reshape(group_count, slices, requests, per_rank, layers, kv_heads, 2)
    factors = factors.transpose(0, 2, 4, 5, 1, 3, 6).reshape(group_count * requests, layers, kv_heads, NB, 2)
    lengths = prompt_len.reshape(-1)
    inside = jnp.arange(PROMPT)[None, :] < lengths[:, None]
    codes = jnp.where(inside[:, None, None, :, None], codes, jnp.zeros((), codes.dtype))
    chosen = dest_group[..., 0]
    matching = chosen[:, :, None] == chosen[:, None, :]
    earlier = jnp.arange(requests)[None, :] < jnp.arange(requests)[:, None]
    arrival_rank = jnp.sum(matching & earlier[None], axis=-1)
    slot_index = (chosen * SLOTS + jnp.arange(group_count)[:, None] * CAPR + arrival_rank).reshape(-1).astype(jnp.int32)
    slot_total = N_SRC * SLOTS
    arrived = jnp.zeros((slot_total, layers, kv_heads, PROMPT, row_width), codes.dtype).at[slot_index].set(codes)
    slot_factor = jnp.zeros((slot_total, layers, kv_heads, NB, 2), factors.dtype).at[slot_index].set(factors)
    slot_len = jnp.zeros((slot_total,), jnp.int32).at[slot_index].set(lengths)
    arrived_cache = arrived.transpose(1, 0, 2, 3, 4)
    halves = arrived_cache.reshape(layers, slot_total, kv_heads, NB, block_len, 2, head_dim).astype(jnp.float32)
    weighting = slot_factor.transpose(1, 0, 2, 3, 4).astype(jnp.float32)[:, :, :, :, None, :, None]
    dequantized = (halves * weighting).astype(jnp.bfloat16).reshape(layers * slot_total, kv_heads, PROMPT, row_width)
    query_view = queries.reshape(layers, N_SRC, ROWS, kv_heads, NEW, queries.shape[-1])
    fresh_view = new_kv.reshape(layers, N_SRC, ROWS, kv_heads, NEW, row_width)
    res_query = query_view[:, :, :RES].reshape(layers * N_SRC * RES, kv_heads, NEW, queries.shape[-1])
    res_fresh = fresh_view[:, :, :RES].reshape(layers * N_SRC * RES, kv_heads, NEW, row_width)
    slot_query = query_view[:, :, RES:].reshape(layers * slot_total, kv_heads, NEW, queries.shape[-1])
    slot_fresh = fresh_view[:, :, RES:].reshape(layers * slot_total, kv_heads, NEW, row_width)
    res_context = res_cache.reshape(layers * N_SRC * RES, kv_heads, CTX, row_width)
    res_lengths = jnp.tile(res_len.reshape(-1), layers)
    slot_lengths = jnp.tile(slot_len, layers)
    res_out = lax.map(one_row, (res_query, res_context, res_lengths, res_fresh))
    slot_out = lax.map(one_row, (slot_query, dequantized, slot_lengths, slot_fresh))
    res_out = res_out.reshape(layers, N_SRC, RES, kv_heads, NEW, queries.shape[-1])
    slot_out = slot_out.reshape(layers, N_SRC, SLOTS, kv_heads, NEW, queries.shape[-1])
    attn_out = jnp.concatenate([res_out, slot_out], axis=2).reshape(layers, N_SRC * ROWS, kv_heads, NEW, queries.shape[-1])
    return attn_out, arrived_cache
```

```python
import functools
import math

import jax
import jax.numpy as jnp
from jax import lax
from jax.experimental import pallas as pl
from jax.experimental.pallas import tpu as pltpu
from jax.sharding import PartitionSpec as P

HEAD = 128
STEPS = 8
GROUP = 16
QUERIES = STEPS * GROUP
TILE = 512
BLOCK = 16
EXPONENT = math.log2(math.e) / math.sqrt(HEAD)
SIZES = (512, 1024, 2048)

KEPT_LEN, KEPT_SLOT, KEPT_REQ = 0, 4, 8
MOVED_LEN, MOVED_SLOT, MOVED_REQ, MOVED_SHIFT = 12, 16, 20, 24
SEND, BRANCH = 28, 32
TABLE = 40


def routes(dest, length):
    count = len(dest)
    same = [[dest[i] == dest[j] for j in range(count)] for i in range(count)]
    one = lambda flag: jnp.where(flag, 1, 0)
    moved, rank = [], []
    for i in range(count):
        flag = jnp.int32(0)
        place = jnp.int32(0)
        for j in range(count):
            if j == i:
                continue
            longer = length[j] >= length[i] if j < i else length[j] > length[i]
            flag = flag + one(jnp.logical_and(same[i][j], longer))
            if j < i:
                place = place + one(same[i][j])
        moved.append(flag > 0)
        rank.append(place)
    free = []
    for plane in range(count):
        named = jnp.int32(0)
        for i in range(count):
            named = named + one(dest[i] == plane)
        free.append(named == 0)
    planes = []
    before = jnp.int32(0)
    for i in range(count):
        choice = jnp.int32(0)
        seen = jnp.int32(0)
        for plane in range(count):
            choice = jnp.where(jnp.logical_and(free[plane], seen == before), plane, choice)
            seen = seen + one(free[plane])
        planes.append(jnp.where(moved[i], choice, dest[i]))
        before = before + one(moved[i])
    return planes, moved, rank


def pack_kernel(me_ref, dest_ref, len_ref, block_ref, pool_ref, out_ref, table_ref, hold, in_sem, out_sem):
    groups, requests = 4, 4
    me = me_ref[0]

    def fetch(n):
        return pltpu.make_async_copy(pool_ref.at[block_ref[n]], hold.at[n], in_sem.at[n])

    for n in range(16):
        fetch(n).start()
    own_planes, _, _ = routes(
        [dest_ref[me * requests + i] for i in range(requests)],
        [len_ref[me * requests + i] for i in range(requests)],
    )

    def place(n):
        rows = pl.ds((n % 4) * BLOCK, BLOCK)
        return pltpu.make_async_copy(hold.at[n], out_ref.at[own_planes[n // 4], :, rows], out_sem.at[n])

    for n in range(16):
        fetch(n).wait()
        place(n).start()

    for n in range(TABLE):
        table_ref[n] = 0
    crowded = jnp.int32(0)
    longest = jnp.int32(0)
    shifts_used = [jnp.int32(0)] * 4
    at_plane = [[jnp.int32(0)] * 4 for _ in range(4)]
    for g in range(groups):
        dest = [dest_ref[g * requests + i] for i in range(requests)]
        length = [len_ref[g * requests + i] for i in range(requests)]
        planes, moved, rank = routes(dest, length)
        for i in range(requests):
            slot = g * 2 + rank[i]
            shift = (dest[i] - planes[i] + 4) & 3
            kept = jnp.logical_and(dest[i] == me, jnp.logical_not(moved[i]))

            @pl.when(kept)
            def _():
                table_ref[KEPT_LEN + g] = length[i]
                table_ref[KEPT_SLOT + g] = slot
                table_ref[KEPT_REQ + g] = g * requests + i

            @pl.when(jnp.logical_and(moved[i], dest[i] == me))
            def _():
                table_ref[MOVED_LEN + g] = length[i]
                table_ref[MOVED_SLOT + g] = slot
                table_ref[MOVED_REQ + g] = g * requests + i
                table_ref[MOVED_SHIFT + g] = shift

            @pl.when(jnp.logical_and(moved[i], planes[i] == me))
            def _():
                table_ref[SEND + shift] = g

            longest = jnp.where(moved[i], jnp.maximum(longest, length[i]), longest)
            for s in range(1, 4):
                hit = jnp.logical_and(moved[i], shift == s)
                shifts_used[s] = jnp.where(hit, 1, shifts_used[s])
                for m in range(4):
                    more = at_plane[m][s] + jnp.where(jnp.logical_and(hit, planes[i] == m), 1, 0)
                    at_plane[m][s] = more
                    crowded = jnp.where(more > 1, 1, crowded)
    kinds = shifts_used[1] + shifts_used[2] + shifts_used[3]
    which = shifts_used[2] + 2 * shifts_used[3]
    size = jnp.int32(0)
    for limit in SIZES[:-1]:
        size = size + jnp.where(longest > limit, 1, 0)
    simple = jnp.logical_and(kinds == 1, crowded == 0)
    table_ref[BRANCH] = jnp.where(simple, 1 + which * len(SIZES) + size, 0)

    for n in range(16):
        place(n).wait()


def pack(me, dest, lengths, blocks, pool):
    smem = pl.BlockSpec(memory_space=pltpu.SMEM)
    hbm = pl.BlockSpec(memory_space=pl.ANY)
    return pl.pallas_call(
        pack_kernel,
        out_shape=(
            jax.ShapeDtypeStruct((4, 32, 4 * BLOCK, 2 * HEAD), jnp.bfloat16),
            jax.ShapeDtypeStruct((TABLE,), jnp.int32),
        ),
        in_specs=[smem, smem, smem, smem, hbm],
        out_specs=(hbm, smem),
        scratch_shapes=[
            pltpu.VMEM((16, 32, BLOCK, 2 * HEAD), jnp.bfloat16),
            pltpu.SemaphoreType.DMA((16,)),
            pltpu.SemaphoreType.DMA((16,)),
        ],
        compiler_params=pltpu.CompilerParams(vmem_limit_bytes=12 << 20),
        cost_estimate=pl.CostEstimate(flops=0, bytes_accessed=8 << 20, transcendentals=0),
        name="pack",
    )(me, dest, lengths, blocks, pool)


def query_rows(query):
    wide = query.astype(jnp.float32)
    return jnp.concatenate([wide[:, q * HEAD : (q + 1) * HEAD] for q in range(GROUP)], axis=0).astype(
        jnp.bfloat16
    )


def against(rows, keys):
    return lax.dot_general(rows, keys, (((1,), (1,)), ((), ())), preferred_element_type=jnp.float32)


def open_row(rows, fresh):
    scores = against(rows, fresh[:, :HEAD])
    step = lax.broadcasted_iota(jnp.int32, scores.shape, 0) & (STEPS - 1)
    key = lax.broadcasted_iota(jnp.int32, scores.shape, 1)
    scores = jnp.where(key <= step, scores, -jnp.inf)
    top = jnp.max(scores, axis=1, keepdims=True)
    weights = jnp.exp2((scores - top) * EXPONENT)
    mass = jnp.sum(weights, axis=1, keepdims=True)
    total = jnp.dot(weights.astype(jnp.bfloat16), fresh[:, HEAD:], preferred_element_type=jnp.float32)
    return top, mass, total


def extend_row(state, rows, keys, values, left):
    top, mass, total = state
    scores = against(rows, keys)
    key = lax.broadcasted_iota(jnp.int32, scores.shape, 1)
    scores = jnp.where(key < left, scores, -jnp.inf)
    higher = jnp.maximum(top, jnp.max(scores, axis=1, keepdims=True))
    fade = jnp.exp2((top - higher) * EXPONENT)
    weights = jnp.exp2((scores - higher) * EXPONENT)
    mass = mass * fade + jnp.sum(weights, axis=1, keepdims=True)
    total = total * fade + jnp.dot(weights.astype(jnp.bfloat16), values, preferred_element_type=jnp.float32)
    return higher, mass, total


def close_row(state):
    _, mass, total = state
    done = total / mass
    return jnp.concatenate([done[q * STEPS : (q + 1) * STEPS] for q in range(GROUP)], axis=1).astype(
        jnp.bfloat16
    )


def resident_kernel(len_ref, table_ref, query_ref, fresh_ref, cache_ref, out_ref, arrived_ref, hold, zeros, in_sem, zero_sem):
    resident, context = cache_ref.shape[0], cache_ref.shape[1]
    tiles = context // TILE
    slots, positions = arrived_ref.shape[0], arrived_ref.shape[1]

    def fetch(r, c):
        part = pl.ds(c * TILE, TILE)
        return pltpu.make_async_copy(cache_ref.at[r, part], hold.at[r, part], in_sem.at[r, c])

    for r in range(resident):
        for c in range(tiles):

            @pl.when(c * TILE < len_ref[r])
            def _():
                fetch(r, c).start()

    def clear(s):
        return pltpu.make_async_copy(zeros, arrived_ref.at[s], zero_sem.at[s])

    zeros[...] = jnp.zeros_like(zeros)
    for s in range(slots):
        clear(s).start()

    def one_row(r, carry):
        rows = query_rows(query_ref[r])
        length = jnp.where(r < resident, len_ref[jnp.minimum(r, resident - 1)], 0)

        def tile(c, state):
            fetch(r, c).wait()
            part = pl.ds(pl.multiple_of(c * TILE, TILE), TILE)
            keys = hold[r, part, :HEAD]
            values = hold[r, part, HEAD:]
            return extend_row(state, rows, keys, values, length - c * TILE)

        state = lax.fori_loop(0, (length + TILE - 1) // TILE, tile, open_row(rows, fresh_ref[r]))
        out_ref[r] = close_row(state)
        return carry

    lax.fori_loop(0, query_ref.shape[0], one_row, 0)
    for s in range(slots):
        clear(s).wait()


def resident(lengths, table, queries, fresh, cache, slots, positions):
    smem = pl.BlockSpec(memory_space=pltpu.SMEM)
    vmem = pl.BlockSpec(memory_space=pltpu.VMEM)
    hbm = pl.BlockSpec(memory_space=pl.ANY)
    rows, context = cache.shape[0], cache.shape[1]
    return pl.pallas_call(
        resident_kernel,
        out_shape=(
            jax.ShapeDtypeStruct(queries.shape, jnp.bfloat16),
            jax.ShapeDtypeStruct((slots, positions, 2 * HEAD), jnp.bfloat16),
        ),
        in_specs=[smem, smem, vmem, vmem, hbm],
        out_specs=(vmem, hbm),
        scratch_shapes=[
            pltpu.VMEM((rows, context, 2 * HEAD), jnp.bfloat16),
            pltpu.VMEM((positions, 2 * HEAD), jnp.bfloat16),
            pltpu.SemaphoreType.DMA((rows, context // TILE)),
            pltpu.SemaphoreType.DMA((slots,)),
        ],
        compiler_params=pltpu.CompilerParams(vmem_limit_bytes=24 << 20),
        cost_estimate=pl.CostEstimate(flops=1 << 31, bytes_accessed=20 << 20, transcendentals=4 << 20),
        name="resident",
    )(lengths, table, queries, fresh, cache)


def slot_kernel(
    first, shared, table_ref, factor_ref, query_ref, fresh_ref, codes_ref, _out, _arrived, out_ref, arrived_ref,
    hold, answer, in_sem, code_sem, answer_sem,
):
    resident = out_ref.shape[0] - query_ref.shape[0]
    tiles = codes_ref.shape[1] // TILE
    groups = 4

    def fetch(g, c):
        part = pl.ds(c * TILE, TILE)
        return pltpu.make_async_copy(
            codes_ref.at[0 if shared else g, part], hold.at[0 if shared else g, part], in_sem.at[0 if shared else g, c]
        )

    def put(g, c):
        part = pl.ds(c * TILE, TILE)
        slot = table_ref[first + 4 + g]
        return pltpu.make_async_copy(
            hold.at[0 if shared else g, part], arrived_ref.at[slot, part], code_sem.at[0 if shared else g, c]
        )

    def reply(g):
        slot = table_ref[first + 4 + g]
        return pltpu.make_async_copy(
            answer.at[0 if shared else g], out_ref.at[resident + slot], answer_sem.at[0 if shared else g]
        )

    for g in range(groups):
        for c in range(tiles):

            @pl.when(c * TILE < table_ref[first + g])
            def _():
                fetch(g, c).start()

    ones = jnp.ones((HEAD, HEAD), jnp.bfloat16)

    def one_slot(g, carry):
        length = table_ref[first + g]
        slot = table_ref[first + 4 + g]
        request = table_ref[first + 8 + g]
        at = 0 if shared else g

        @pl.when(length > 0)
        def _():
            rows = query_rows(query_ref[slot])
            key_factor = factor_ref[pl.ds(2 * request, 1), :]
            value_factor = factor_ref[pl.ds(2 * request + 1, 1), :]

            def tile(c, state):
                fetch(g, c).wait()
                part = pl.ds(pl.multiple_of(c * TILE, TILE), TILE)
                left = length - c * TILE

                @pl.when(left < TILE)
                def _():
                    codes = hold[at, part, :]
                    place = lax.broadcasted_iota(jnp.int32, codes.shape, 0)
                    hold[at, part, :] = jnp.where(place < left, codes.astype(jnp.float32), 0.0).astype(jnp.bfloat16)

                put(g, c).start()
                row = lax.broadcasted_iota(jnp.int32, (TILE, HEAD), 0)
                column = lax.broadcasted_iota(jnp.int32, (TILE, HEAD), 1)
                hit = column == row // BLOCK + c * (TILE // BLOCK)

                def scaled(codes, factor):
                    spread = jnp.where(hit, factor, 0.0).astype(jnp.bfloat16)
                    wide = jnp.dot(spread, ones, preferred_element_type=jnp.float32)
                    return (codes.astype(jnp.float32) * wide).astype(jnp.bfloat16)

                keys = scaled(hold[at, part, :HEAD], key_factor)
                values = scaled(hold[at, part, HEAD:], value_factor)
                return extend_row(state, rows, keys, values, left)

            state = lax.fori_loop(0, (length + TILE - 1) // TILE, tile, open_row(rows, fresh_ref[slot]))
            answer[at] = close_row(state)
            reply(g).start()

        return carry

    lax.fori_loop(0, groups, one_slot, 0)
    for g in range(groups):

        @pl.when(table_ref[first + g] > 0)
        def _():
            reply(g).wait()

        for c in range(tiles):

            @pl.when(c * TILE < table_ref[first + g])
            def _():
                put(g, c).wait()


def fill_slots(first, shared, table, factors, queries, fresh, codes, out, arrived):
    smem = pl.BlockSpec(memory_space=pltpu.SMEM)
    vmem = pl.BlockSpec(memory_space=pltpu.VMEM)
    hbm = pl.BlockSpec(memory_space=pl.ANY)
    slots = arrived.shape[0]
    entries, positions = codes.shape[0], codes.shape[1]
    tail = lambda width: pl.BlockSpec((slots, STEPS, width), lambda n: (1, 0, 0))
    return pl.pallas_call(
        functools.partial(slot_kernel, first, shared),
        grid=(1,),
        out_shape=(
            jax.ShapeDtypeStruct(out.shape, out.dtype),
            jax.ShapeDtypeStruct(arrived.shape, arrived.dtype),
        ),
        in_specs=[smem, vmem, tail(queries.shape[-1]), tail(2 * HEAD), hbm, hbm, hbm],
        out_specs=(hbm, hbm),
        input_output_aliases={5: 0, 6: 1},
        scratch_shapes=[
            pltpu.VMEM((entries, positions, 2 * HEAD), jnp.bfloat16),
            pltpu.VMEM((entries, STEPS, queries.shape[-1]), jnp.bfloat16),
            pltpu.SemaphoreType.DMA((entries, positions // TILE)),
            pltpu.SemaphoreType.DMA((entries, positions // TILE)),
            pltpu.SemaphoreType.DMA((entries,)),
        ],
        compiler_params=pltpu.CompilerParams(vmem_limit_bytes=16 << 20),
        cost_estimate=pl.CostEstimate(flops=1 << 30, bytes_accessed=8 << 20, transcendentals=1 << 20),
        name="moved_slots" if first == MOVED_LEN else "kept_slots",
    )(table, factors, queries, fresh, codes, out, arrived)


def shifted(values, shift):
    return lax.ppermute(values, "src", [(g, (g + shift) % 4) for g in range(4)])


def on_device(
    prefill_pool,
    block_scales,
    block_table,
    prompt_len,
    dest_group,
    res_len,
    res_cache,
    queries,
    new_kv,
):
    everywhere = ("src", "section", "tp")
    me = lax.axis_index("src").astype(jnp.int32).reshape(1)
    layer_head = lax.axis_index(("section", "tp"))
    layers, heads, block_len, width = prefill_pool.shape[4:]
    pool = prefill_pool.reshape(16, layers * heads, block_len, width)
    slots = queries.shape[1] - res_cache.shape[1]
    positions = 32 * 4 * block_len
    query_view, fresh_view = queries[0, :, 0], new_kv[0, :, 0]

    packed, table = pack(me, dest_group.reshape(-1), prompt_len.reshape(-1), block_table.reshape(-1), pool)
    landed = lax.all_to_all(
        packed.reshape(128, 4 * block_len, width), everywhere, split_axis=0, concat_axis=0, tiled=True
    ).reshape(4, positions, width)

    out, arrived = resident(res_len.reshape(-1), table, query_view, fresh_view, res_cache[0, :, 0], slots, positions)

    scales = jnp.take(block_scales.reshape(16, layers * heads, 2), block_table.reshape(-1), axis=0)
    scales = scales.transpose(1, 0, 2).reshape(8, 128)
    scales = lax.all_gather(scales, everywhere, axis=0, tiled=True).reshape(128, 32, 32)
    scales = lax.dynamic_index_in_dim(scales, layer_head, axis=1, keepdims=False)
    factors = scales.reshape(4, 32, 4, 4, 2).transpose(0, 2, 4, 1, 3).reshape(32, 128).astype(jnp.float32)

    def kept(landed, out, arrived):
        return fill_slots(KEPT_LEN, False, table, factors, query_view, fresh_view, landed, out, arrived)

    def moved(shared, codes, out, arrived):
        return fill_slots(MOVED_LEN, shared, table, factors, query_view, fresh_view, codes, out, arrived)

    def general(landed, out, arrived):
        codes = jnp.zeros_like(landed)
        for shift in range(1, 4):
            hit = table[MOVED_SHIFT : MOVED_SHIFT + 4] == shift
            codes = jnp.where(hit[:, None, None], shifted(landed, shift), codes)
        out, arrived = kept(landed, out, arrived)
        return moved(False, codes, out, arrived)

    def direct(shift, size, landed, out, arrived):
        leaving = lax.dynamic_slice(landed, (table[SEND + shift], 0, 0), (1, size, width))
        codes = shifted(leaving, shift)
        out, arrived = kept(landed, out, arrived)
        return moved(True, codes, out, arrived)

    branches = [general] + [
        functools.partial(direct, shift, size) for shift in range(1, 4) for size in SIZES
    ]
    out, arrived = lax.switch(table[BRANCH], branches, landed, out, arrived)
    return out[None, :, None], arrived[None, :, None]


def solution(mesh):
    return jax.shard_map(
        on_device,
        mesh=mesh,
        in_specs=(
            P("src", "section", "tp", None, None, None, None, None),
            P("src", "section", "tp", None, None, None, None),
            P("src", "section", "tp", None),
            P(),
            P(),
            P("src", None),
            P("section", "src", "tp", None, None),
            P("section", "src", "tp", None, None),
            P("section", "src", "tp", None, None),
        ),
        out_specs=(P("section", "src", "tp", None, None), P("section", "src", "tp", None, None)),
        check_vma=False,
    )
```

```python
import functools
import math

import jax
import jax.numpy as jnp
from jax import lax
from jax.experimental import pallas as pl
from jax.experimental.pallas import tpu as pltpu
from jax.sharding import PartitionSpec as P

HEAD = 128
STEPS = 8
GROUP = 16
QUERIES = STEPS * GROUP
TILE = 512
BLOCK = 16
EXPONENT = math.log2(math.e) / math.sqrt(HEAD)
SIZES = (512, 1024, 2048)
VMEM = 63_200_000

KEPT_LEN, KEPT_SLOT, KEPT_REQ = 0, 4, 8
MOVED_LEN, MOVED_SLOT, MOVED_REQ, MOVED_SHIFT = 12, 16, 20, 24
SEND, BRANCH, POOL = 28, 32, 40
TABLE = 56


def routes(dest, length):
    count = len(dest)
    same = [[dest[i] == dest[j] for j in range(count)] for i in range(count)]
    one = lambda flag: jnp.where(flag, 1, 0)
    moved, rank = [], []
    for i in range(count):
        flag = jnp.int32(0)
        place = jnp.int32(0)
        for j in range(count):
            if j == i:
                continue
            longer = length[j] >= length[i] if j < i else length[j] > length[i]
            flag = flag + one(jnp.logical_and(same[i][j], longer))
            if j < i:
                place = place + one(same[i][j])
        moved.append(flag > 0)
        rank.append(place)
    free = []
    for plane in range(count):
        named = jnp.int32(0)
        for i in range(count):
            named = named + one(dest[i] == plane)
        free.append(named == 0)
    planes = []
    before = jnp.int32(0)
    for i in range(count):
        choice = jnp.int32(0)
        seen = jnp.int32(0)
        for plane in range(count):
            choice = jnp.where(jnp.logical_and(free[plane], seen == before), plane, choice)
            seen = seen + one(free[plane])
        planes.append(jnp.where(moved[i], choice, dest[i]))
        before = before + one(moved[i])
    return planes, moved, rank


def pack_kernel(me_ref, dest_ref, len_ref, block_ref, pool_ref, out_ref, table_ref, hold, in_sem, out_sem):
    groups, requests = 4, 4
    me = me_ref[0]

    def fetch(n):
        return pltpu.make_async_copy(pool_ref.at[block_ref[0, 0, 0, n]], hold.at[n], in_sem.at[n])

    for n in range(16):
        fetch(n).start()
    own_planes, _, _ = routes(
        [dest_ref[me, 0, i] for i in range(requests)],
        [len_ref[me, i] for i in range(requests)],
    )

    def place(n):
        rows = pl.ds((n % 4) * BLOCK, BLOCK)
        return pltpu.make_async_copy(hold.at[n], out_ref.at[own_planes[n // 4], :, rows], out_sem.at[n])

    for n in range(16):
        fetch(n).wait()
        place(n).start()

    for n in range(POOL):
        table_ref[n] = 0
    for n in range(16):
        table_ref[POOL + n] = block_ref[0, 0, 0, n]
    crowded = jnp.int32(0)
    longest = jnp.int32(0)
    shifts_used = [jnp.int32(0)] * 4
    at_plane = [[jnp.int32(0)] * 4 for _ in range(4)]
    for g in range(groups):
        dest = [dest_ref[g, 0, i] for i in range(requests)]
        length = [len_ref[g, i] for i in range(requests)]
        planes, moved, rank = routes(dest, length)
        for i in range(requests):
            slot = g * 2 + rank[i]
            shift = (dest[i] - planes[i] + 4) & 3
            kept = jnp.logical_and(dest[i] == me, jnp.logical_not(moved[i]))

            @pl.when(kept)
            def _():
                table_ref[KEPT_LEN + g] = length[i]
                table_ref[KEPT_SLOT + g] = slot
                table_ref[KEPT_REQ + g] = g * requests + i

            @pl.when(jnp.logical_and(moved[i], dest[i] == me))
            def _():
                table_ref[MOVED_LEN + g] = length[i]
                table_ref[MOVED_SLOT + g] = slot
                table_ref[MOVED_REQ + g] = g * requests + i
                table_ref[MOVED_SHIFT + g] = shift

            @pl.when(jnp.logical_and(moved[i], planes[i] == me))
            def _():
                table_ref[SEND + shift] = g

            longest = jnp.where(moved[i], jnp.maximum(longest, length[i]), longest)
            for s in range(1, 4):
                hit = jnp.logical_and(moved[i], shift == s)
                shifts_used[s] = jnp.where(hit, 1, shifts_used[s])
                for m in range(4):
                    more = at_plane[m][s] + jnp.where(jnp.logical_and(hit, planes[i] == m), 1, 0)
                    at_plane[m][s] = more
                    crowded = jnp.where(more > 1, 1, crowded)
    kinds = shifts_used[1] + shifts_used[2] + shifts_used[3]
    which = shifts_used[2] + 2 * shifts_used[3]
    size = jnp.int32(0)
    for limit in SIZES[:-1]:
        size = size + jnp.where(longest > limit, 1, 0)
    simple = jnp.logical_and(kinds == 1, crowded == 0)
    table_ref[BRANCH] = jnp.where(simple, 1 + which * len(SIZES) + size, 0)

    for n in range(16):
        place(n).wait()


def pack(me, dest, lengths, blocks, pool):
    smem = pl.BlockSpec(memory_space=pltpu.SMEM)
    hbm = pl.BlockSpec(memory_space=pltpu.HBM)
    return pl.pallas_call(
        pack_kernel,
        out_shape=(
            jax.ShapeDtypeStruct((4, 32, 4 * BLOCK, 2 * HEAD), jnp.bfloat16),
            jax.ShapeDtypeStruct((TABLE,), jnp.int32),
        ),
        in_specs=[smem, smem, smem, smem, hbm],
        out_specs=(hbm, smem),
        scratch_shapes=[
            pltpu.VMEM((16, 32, BLOCK, 2 * HEAD), jnp.bfloat16),
            pltpu.SemaphoreType.DMA((16,)),
            pltpu.SemaphoreType.DMA((16,)),
        ],
        compiler_params=pltpu.CompilerParams(vmem_limit_bytes=VMEM),
        cost_estimate=pl.CostEstimate(flops=0, bytes_accessed=8 << 20, transcendentals=0),
        name="pack",
    )(me, dest, lengths, blocks, pool)


def query_rows(query):
    wide = query.astype(jnp.float32)
    return jnp.concatenate([wide[:, q * HEAD : (q + 1) * HEAD] for q in range(GROUP)], axis=0).astype(
        jnp.bfloat16
    )


def against(rows, keys):
    return lax.dot_general(rows, keys, (((1,), (1,)), ((), ())), preferred_element_type=jnp.float32)


def open_row(rows, fresh):
    scores = against(rows, fresh[:, :HEAD])
    step = lax.broadcasted_iota(jnp.int32, scores.shape, 0) & (STEPS - 1)
    key = lax.broadcasted_iota(jnp.int32, scores.shape, 1)
    scores = jnp.where(key <= step, scores, -jnp.inf)
    top = jnp.max(scores, axis=1, keepdims=True)
    weights = jnp.exp2((scores - top) * EXPONENT)
    mass = jnp.sum(weights, axis=1, keepdims=True)
    total = jnp.dot(weights.astype(jnp.bfloat16), fresh[:, HEAD:], preferred_element_type=jnp.float32)
    return top, mass, total


def extend_row(state, rows, keys, values, left):
    top, mass, total = state
    scores = against(rows, keys)
    key = lax.broadcasted_iota(jnp.int32, scores.shape, 1)
    scores = jnp.where(key < left, scores, -jnp.inf)
    higher = jnp.maximum(top, jnp.max(scores, axis=1, keepdims=True))
    fade = jnp.exp2((top - higher) * EXPONENT)
    weights = jnp.exp2((scores - higher) * EXPONENT)
    mass = mass * fade + jnp.sum(weights, axis=1, keepdims=True)
    total = total * fade + jnp.dot(weights.astype(jnp.bfloat16), values, preferred_element_type=jnp.float32)
    return higher, mass, total


def close_row(state):
    _, mass, total = state
    done = total / mass
    return jnp.concatenate([done[q * STEPS : (q + 1) * STEPS] for q in range(GROUP)], axis=1).astype(
        jnp.bfloat16
    )


def resident_kernel(len_ref, table_ref, query_ref, fresh_ref, cache_ref, out_ref, arrived_ref, pool_ref, hold, zeros, in_sem, zero_sem):
    resident, context = cache_ref.shape[0], cache_ref.shape[1]
    tiles = context // TILE
    slots, positions = arrived_ref.shape[0], arrived_ref.shape[1]

    def fetch(r, c):
        part = pl.ds(c * TILE, TILE)
        return pltpu.make_async_copy(cache_ref.at[r, part], hold.at[r, part], in_sem.at[r, c])

    for r in range(resident):
        for c in range(tiles):

            @pl.when(c * TILE < len_ref[0, r])
            def _():
                fetch(r, c).start()

    def clear(s):
        return pltpu.make_async_copy(zeros, arrived_ref.at[s], zero_sem.at[s])

    for n in range(16):
        pool_ref[n] = table_ref[POOL + n]
    zeros[...] = jnp.zeros_like(zeros)
    for s in range(slots):
        clear(s).start()

    def one_row(r, carry):
        rows = query_rows(query_ref[r])
        length = jnp.where(r < resident, len_ref[0, jnp.minimum(r, resident - 1)], 0)

        def tile(c, state):
            fetch(r, c).wait()
            part = pl.ds(pl.multiple_of(c * TILE, TILE), TILE)
            keys = hold[r, part, :HEAD]
            values = hold[r, part, HEAD:]
            return extend_row(state, rows, keys, values, length - c * TILE)

        state = lax.fori_loop(0, (length + TILE - 1) // TILE, tile, open_row(rows, fresh_ref[r]))
        out_ref[r] = close_row(state)
        return carry

    lax.fori_loop(0, query_ref.shape[0], one_row, 0)
    for s in range(slots):
        clear(s).wait()


def resident(lengths, table, queries, fresh, cache, slots, positions):
    smem = pl.BlockSpec(memory_space=pltpu.SMEM)
    vmem = pl.BlockSpec(memory_space=pltpu.VMEM)
    hbm = pl.BlockSpec(memory_space=pltpu.HBM)
    rows, context = cache.shape[0], cache.shape[1]
    return pl.pallas_call(
        resident_kernel,
        out_shape=(
            jax.ShapeDtypeStruct(queries.shape, jnp.bfloat16),
            jax.ShapeDtypeStruct((slots, positions, 2 * HEAD), jnp.bfloat16),
            jax.ShapeDtypeStruct((16,), jnp.int32),
        ),
        in_specs=[smem, smem, vmem, vmem, hbm],
        out_specs=(vmem, hbm, smem),
        scratch_shapes=[
            pltpu.VMEM((rows, context, 2 * HEAD), jnp.bfloat16),
            pltpu.VMEM((positions, 2 * HEAD), jnp.bfloat16),
            pltpu.SemaphoreType.DMA((rows, context // TILE)),
            pltpu.SemaphoreType.DMA((slots,)),
        ],
        compiler_params=pltpu.CompilerParams(vmem_limit_bytes=VMEM),
        cost_estimate=pl.CostEstimate(flops=1 << 31, bytes_accessed=20 << 20, transcendentals=4 << 20),
        name="resident",
    )(lengths, table, queries, fresh, cache)


def slot_kernel(
    first, shared, table_ref, factor_ref, query_ref, fresh_ref, codes_ref, _out, _arrived, out_ref, arrived_ref,
    hold, answer, in_sem, code_sem, answer_sem,
):
    resident = out_ref.shape[0] - query_ref.shape[0]
    positions = codes_ref.shape[1]
    tiles = pl.cdiv(positions, TILE)
    groups = 4

    def fetch(g, c):
        part = pl.ds(c * TILE, min(TILE, positions - c * TILE))
        return pltpu.make_async_copy(
            codes_ref.at[0 if shared else g, part], hold.at[0 if shared else g, part], in_sem.at[0 if shared else g, c]
        )

    def put(g, c):
        part = pl.ds(c * TILE, TILE)
        slot = table_ref[first + 4 + g]
        return pltpu.make_async_copy(
            hold.at[0 if shared else g, part], arrived_ref.at[slot, part], code_sem.at[0 if shared else g, c]
        )

    def reply(g):
        slot = table_ref[first + 4 + g]
        return pltpu.make_async_copy(
            answer.at[0 if shared else g], out_ref.at[resident + slot], answer_sem.at[0 if shared else g]
        )

    for g in range(groups):
        for c in range(tiles):

            @pl.when(c * TILE < table_ref[first + g])
            def _():
                fetch(g, c).start()

    ones = jnp.ones((HEAD, HEAD), jnp.bfloat16)

    def one_slot(g, carry):
        length = table_ref[first + g]
        slot = table_ref[first + 4 + g]
        request = table_ref[first + 8 + g]
        at = 0 if shared else g

        @pl.when(length > 0)
        def _():
            rows = query_rows(query_ref[slot])
            key_factor = factor_ref[pl.ds(2 * request, 1), :]
            value_factor = factor_ref[pl.ds(2 * request + 1, 1), :]

            def tile(c, state):
                for n in range(tiles):

                    @pl.when(c == n)
                    def _():
                        fetch(g, n).wait()

                part = pl.ds(pl.multiple_of(c * TILE, TILE), TILE)
                left = length - c * TILE

                @pl.when(left < TILE)
                def _():
                    codes = hold[at, part, :]
                    place = lax.broadcasted_iota(jnp.int32, codes.shape, 0)
                    hold[at, part, :] = jnp.where(place < left, codes.astype(jnp.float32), 0.0).astype(jnp.bfloat16)

                put(g, c).start()
                row = lax.broadcasted_iota(jnp.int32, (TILE, HEAD), 0)
                column = lax.broadcasted_iota(jnp.int32, (TILE, HEAD), 1)
                hit = column == row // BLOCK + c * (TILE // BLOCK)

                def scaled(codes, factor):
                    spread = jnp.where(hit, factor, 0.0).astype(jnp.bfloat16)
                    wide = jnp.dot(spread, ones, preferred_element_type=jnp.float32)
                    return (codes.astype(jnp.float32) * wide).astype(jnp.bfloat16)

                keys = scaled(hold[at, part, :HEAD], key_factor)
                values = scaled(hold[at, part, HEAD:], value_factor)
                return extend_row(state, rows, keys, values, left)

            state = lax.fori_loop(0, (length + TILE - 1) // TILE, tile, open_row(rows, fresh_ref[slot]))
            answer[at] = close_row(state)
            reply(g).start()

        return carry

    lax.fori_loop(0, groups, one_slot, 0)
    for g in range(groups):

        @pl.when(table_ref[first + g] > 0)
        def _():
            reply(g).wait()

        for c in range(tiles):

            @pl.when(c * TILE < table_ref[first + g])
            def _():
                put(g, c).wait()


def fill_slots(first, shared, table, factors, queries, fresh, codes, out, arrived):
    smem = pl.BlockSpec(memory_space=pltpu.SMEM)
    vmem = pl.BlockSpec(memory_space=pltpu.VMEM)
    hbm = pl.BlockSpec(memory_space=pltpu.HBM)
    slots = arrived.shape[0]
    entries, tiles = codes.shape[0], pl.cdiv(codes.shape[1], TILE)
    tail = lambda width: pl.BlockSpec((slots, STEPS, width), lambda n: (1, 0, 0))
    return pl.pallas_call(
        functools.partial(slot_kernel, first, shared),
        grid=(1,),
        out_shape=(
            jax.ShapeDtypeStruct(out.shape, out.dtype),
            jax.ShapeDtypeStruct(arrived.shape, arrived.dtype),
        ),
        in_specs=[smem, vmem, tail(queries.shape[-1]), tail(2 * HEAD), hbm, hbm, hbm],
        out_specs=(hbm, hbm),
        input_output_aliases={5: 0, 6: 1},
        scratch_shapes=[
            pltpu.VMEM((entries, tiles * TILE, 2 * HEAD), jnp.bfloat16),
            pltpu.VMEM((entries, STEPS, queries.shape[-1]), jnp.bfloat16),
            pltpu.SemaphoreType.DMA((entries, tiles)),
            pltpu.SemaphoreType.DMA((entries, tiles)),
            pltpu.SemaphoreType.DMA((entries,)),
        ],
        compiler_params=pltpu.CompilerParams(vmem_limit_bytes=VMEM),
        cost_estimate=pl.CostEstimate(flops=1 << 30, bytes_accessed=8 << 20, transcendentals=1 << 20),
        name="moved_slots" if first == MOVED_LEN else "kept_slots",
    )(table, factors, queries, fresh, codes, out, arrived)


def leave_kernel(shift, table_ref, codes_ref, out_ref, sem):
    rows = pl.ds(0, out_ref.shape[0])
    copy = pltpu.make_async_copy(codes_ref.at[table_ref[SEND + shift], rows], out_ref, sem)
    copy.start()
    copy.wait()


def leave(shift, size, table, codes):
    return pl.pallas_call(
        functools.partial(leave_kernel, shift),
        out_shape=jax.ShapeDtypeStruct((size, codes.shape[2]), codes.dtype),
        in_specs=[pl.BlockSpec(memory_space=pltpu.SMEM), pl.BlockSpec(memory_space=pl.ANY)],
        out_specs=pl.BlockSpec(memory_space=pltpu.VMEM),
        scratch_shapes=[pltpu.SemaphoreType.DMA],
        compiler_params=pltpu.CompilerParams(vmem_limit_bytes=VMEM),
        name="leave",
    )(table, codes)


def shifted(values, shift):
    return lax.ppermute(values, "src", [(g, (g + shift) % 4) for g in range(4)])


def on_device(
    prefill_pool,
    block_scales,
    block_table,
    prompt_len,
    dest_group,
    res_len,
    res_cache,
    queries,
    new_kv,
):
    everywhere = ("src", "section", "tp")
    me = lax.axis_index("src").astype(jnp.int32).reshape(1)
    layers, heads, block_len, width = prefill_pool.shape[4:]
    pool = prefill_pool.reshape(16, layers * heads, block_len, width)
    slots = queries.shape[1] - res_cache.shape[1]
    positions = 32 * 4 * block_len
    query_view, fresh_view = queries[0, :, 0], new_kv[0, :, 0]

    packed, table = pack(me, dest_group.transpose(0, 2, 1), prompt_len, block_table, pool)
    landed = lax.all_to_all(
        packed.reshape(128, 4 * block_len, width), everywhere, split_axis=0, concat_axis=0, tiled=True
    ).reshape(4, positions, width)

    out, arrived, taken = resident(res_len, table, query_view, fresh_view, res_cache[0, :, 0], slots, positions)

    taken = (jnp.arange(16)[:, None] == taken[None, :]).astype(jnp.bfloat16)
    scales = block_scales.reshape(16, layers * heads, 2).transpose(1, 2, 0).reshape(64, 16)
    scales = jnp.dot(scales, taken, preferred_element_type=jnp.float32).astype(jnp.bfloat16)
    scales = jnp.tile(scales.reshape(1, 32, 32), (4, 1, 1)).reshape(128, 32)
    scales = lax.all_to_all(scales, everywhere, split_axis=0, concat_axis=0, tiled=True)
    factors = scales.reshape(4, 32, 2, 4, 4).transpose(0, 3, 2, 1, 4).reshape(32, 128).astype(jnp.float32)

    def kept(landed, out, arrived):
        return fill_slots(KEPT_LEN, False, table, factors, query_view, fresh_view, landed, out, arrived)

    def moved(shared, codes, out, arrived):
        return fill_slots(MOVED_LEN, shared, table, factors, query_view, fresh_view, codes, out, arrived)

    def general(landed, out, arrived):
        codes = jnp.zeros_like(landed)
        for shift in range(1, 4):
            hit = table[MOVED_SHIFT : MOVED_SHIFT + 4] == shift
            codes = jnp.where(hit[:, None, None], shifted(landed, shift), codes)
        out, arrived = kept(landed, out, arrived)
        return moved(False, codes, out, arrived)

    def direct(shift, size, landed, out, arrived):
        codes = shifted(leave(shift, size, table, landed), shift)[None]
        out, arrived = kept(landed, out, arrived)
        return moved(True, codes, out, arrived)

    branches = [general] + [
        functools.partial(direct, shift, size) for shift in range(1, 4) for size in SIZES
    ]
    out, arrived = lax.switch(table[BRANCH], branches, landed, out, arrived)
    return out[None, :, None], arrived[None, :, None]


def solution(mesh):
    return jax.shard_map(
        on_device,
        mesh=mesh,
        in_specs=(
            P("src", "section", "tp", None, None, None, None, None),
            P("src", "section", "tp", None, None, None, None),
            P("src", "section", "tp", None),
            P(),
            P(),
            P("src", None),
            P("section", "src", "tp", None, None),
            P("section", "src", "tp", None, None),
            P("section", "src", "tp", None, None),
        ),
        out_specs=(P("section", "src", "tp", None, None), P("section", "src", "tp", None, None)),
        check_vma=False,
    )
```

```python
import functools
import math

import jax
import jax.numpy as jnp
from jax import lax
from jax.experimental import pallas as pl
from jax.experimental.pallas import tpu as pltpu
from jax.sharding import PartitionSpec as P

HEAD = 128
STEPS = 8
GROUP = 16
QUERIES = STEPS * GROUP
TILE = 512
BLOCK = 16
CHUNK = 4 * BLOCK
SPAN = TILE // CHUNK
FACTORS = 2 * CHUNK
CHUNK_ROWS = 2 * CHUNK + 8
EXPONENT = math.log2(math.e) / math.sqrt(HEAD)
SIZES = (512, 1024, 1536, 2048)
VMEM = 63_200_000

KEPT_LEN, KEPT_SLOT = 0, 4
MOVED_LEN, MOVED_SLOT, MOVED_SHIFT = 8, 12, 16
SEND, BRANCH = 20, 24
TABLE = 32


def routes(dest, length):
    count = len(dest)
    same = [[dest[i] == dest[j] for j in range(count)] for i in range(count)]
    one = lambda flag: jnp.where(flag, 1, 0)
    moved, rank = [], []
    for i in range(count):
        flag = jnp.int32(0)
        place = jnp.int32(0)
        for j in range(count):
            if j == i:
                continue
            longer = length[j] >= length[i] if j < i else length[j] > length[i]
            flag = flag + one(jnp.logical_and(same[i][j], longer))
            if j < i:
                place = place + one(same[i][j])
        moved.append(flag > 0)
        rank.append(place)
    free = []
    for plane in range(count):
        named = jnp.int32(0)
        for i in range(count):
            named = named + one(dest[i] == plane)
        free.append(named == 0)
    planes = []
    before = jnp.int32(0)
    for i in range(count):
        choice = jnp.int32(0)
        seen = jnp.int32(0)
        for plane in range(count):
            choice = jnp.where(jnp.logical_and(free[plane], seen == before), plane, choice)
            seen = seen + one(free[plane])
        planes.append(jnp.where(moved[i], choice, dest[i]))
        before = before + one(moved[i])
    return planes, moved, rank


def pack_kernel(
    me_ref, dest_ref, len_ref, block_ref, scale_ref, pool_ref, out_ref, table_ref,
    hold, wide, in_sem, key_sem, value_sem, wide_sem,
):
    groups, requests = 4, 4
    me = me_ref[0]

    def fetch(n):
        return pltpu.make_async_copy(pool_ref.at[block_ref[0, 0, 0, n]], hold.at[n], in_sem.at[n])

    for n in range(16):
        fetch(n).start()
    own_planes, _, _ = routes(
        [dest_ref[me, 0, i] for i in range(requests)],
        [len_ref[me, i] for i in range(requests)],
    )

    def place(n):
        block = (n % 4) * BLOCK
        keys = out_ref.at[own_planes[n // 4], :, pl.ds(block, BLOCK)]
        values = out_ref.at[own_planes[n // 4], :, pl.ds(CHUNK + block, BLOCK)]
        return (
            pltpu.make_async_copy(hold.at[n, :, :, pl.ds(0, HEAD)], keys, key_sem.at[n]),
            pltpu.make_async_copy(hold.at[n, :, :, pl.ds(HEAD, HEAD)], values, value_sem.at[n]),
        )

    def place_factors(i):
        rows = out_ref.at[own_planes[i], :, pl.ds(FACTORS, 8)]
        return pltpu.make_async_copy(wide.at[i], rows, wide_sem.at[i])

    scales = scale_ref[...].astype(jnp.float32)
    block = (lax.broadcasted_iota(jnp.int32, scales.shape, 0) >> 1) & 3
    entry = lax.broadcasted_iota(jnp.int32, scales.shape, 1)
    ones = jnp.ones((scales.shape[1], HEAD), jnp.bfloat16)
    for i in range(requests):
        wanted = jnp.full(scales.shape, block_ref[0, 0, 0, 4 * i], jnp.int32)
        for k in range(1, 4):
            wanted = jnp.where(block == k, block_ref[0, 0, 0, 4 * i + k], wanted)
        picked = jnp.where(entry == wanted, scales, 0.0).astype(jnp.bfloat16)
        spread = jnp.dot(picked, ones, preferred_element_type=jnp.float32)
        wide[i] = spread.reshape(wide.shape[1:]).astype(jnp.bfloat16)
        place_factors(i).start()

    for n in range(16):
        fetch(n).wait()
        for copy in place(n):
            copy.start()

    for n in range(TABLE):
        table_ref[n] = 0
    crowded = jnp.int32(0)
    longest = jnp.int32(0)
    shifts_used = [jnp.int32(0)] * 4
    at_plane = [[jnp.int32(0)] * 4 for _ in range(4)]
    for g in range(groups):
        dest = [dest_ref[g, 0, i] for i in range(requests)]
        length = [len_ref[g, i] for i in range(requests)]
        planes, moved, rank = routes(dest, length)
        for i in range(requests):
            slot = g * 2 + rank[i]
            shift = (dest[i] - planes[i] + 4) & 3
            kept = jnp.logical_and(dest[i] == me, jnp.logical_not(moved[i]))

            @pl.when(kept)
            def _():
                table_ref[KEPT_LEN + g] = length[i]
                table_ref[KEPT_SLOT + g] = slot

            @pl.when(jnp.logical_and(moved[i], dest[i] == me))
            def _():
                table_ref[MOVED_LEN + g] = length[i]
                table_ref[MOVED_SLOT + g] = slot
                table_ref[MOVED_SHIFT + g] = shift

            @pl.when(jnp.logical_and(moved[i], planes[i] == me))
            def _():
                table_ref[SEND + shift] = g

            longest = jnp.where(moved[i], jnp.maximum(longest, length[i]), longest)
            for s in range(1, 4):
                hit = jnp.logical_and(moved[i], shift == s)
                shifts_used[s] = jnp.where(hit, 1, shifts_used[s])
                for m in range(4):
                    more = at_plane[m][s] + jnp.where(jnp.logical_and(hit, planes[i] == m), 1, 0)
                    at_plane[m][s] = more
                    crowded = jnp.where(more > 1, 1, crowded)
    kinds = shifts_used[1] + shifts_used[2] + shifts_used[3]
    which = shifts_used[2] + 2 * shifts_used[3]
    size = jnp.int32(0)
    for limit in SIZES[:-1]:
        size = size + jnp.where(longest > limit, 1, 0)
    simple = jnp.logical_and(kinds == 1, crowded == 0)
    table_ref[BRANCH] = jnp.where(simple, 1 + which * len(SIZES) + size, 0)

    for n in range(16):
        for copy in place(n):
            copy.wait()
    for i in range(requests):
        place_factors(i).wait()


def pack(me, dest, lengths, blocks, scales, pool):
    smem = pl.BlockSpec(memory_space=pltpu.SMEM)
    vmem = pl.BlockSpec(memory_space=pltpu.VMEM)
    hbm = pl.BlockSpec(memory_space=pltpu.HBM)
    return pl.pallas_call(
        pack_kernel,
        out_shape=(
            jax.ShapeDtypeStruct((4, 32, CHUNK_ROWS, HEAD), jnp.bfloat16),
            jax.ShapeDtypeStruct((TABLE,), jnp.int32),
        ),
        in_specs=[smem, smem, smem, smem, vmem, hbm],
        out_specs=(hbm, smem),
        scratch_shapes=[
            pltpu.VMEM((16, 32, BLOCK, 2 * HEAD), jnp.bfloat16),
            pltpu.VMEM((4, 32, 8, HEAD), jnp.bfloat16),
            pltpu.SemaphoreType.DMA((16,)),
            pltpu.SemaphoreType.DMA((16,)),
            pltpu.SemaphoreType.DMA((16,)),
            pltpu.SemaphoreType.DMA((4,)),
        ],
        compiler_params=pltpu.CompilerParams(vmem_limit_bytes=VMEM),
        cost_estimate=pl.CostEstimate(flops=0, bytes_accessed=8 << 20, transcendentals=0),
        name="pack",
    )(me, dest, lengths, blocks, scales, pool)


def query_rows(query):
    wide = query.astype(jnp.float32)
    return jnp.concatenate([wide[:, q * HEAD : (q + 1) * HEAD] for q in range(GROUP)], axis=0).astype(
        jnp.bfloat16
    )


def against(rows, keys):
    return lax.dot_general(rows, keys, (((1,), (1,)), ((), ())), preferred_element_type=jnp.float32)


def open_row(rows, fresh):
    scores = against(rows, fresh[:, :HEAD])
    step = lax.broadcasted_iota(jnp.int32, scores.shape, 0) & (STEPS - 1)
    key = lax.broadcasted_iota(jnp.int32, scores.shape, 1)
    scores = jnp.where(key <= step, scores, -jnp.inf)
    top = jnp.max(scores, axis=1, keepdims=True)
    weights = jnp.exp2((scores - top) * EXPONENT)
    mass = jnp.sum(weights, axis=1, keepdims=True)
    total = jnp.dot(weights.astype(jnp.bfloat16), fresh[:, HEAD:], preferred_element_type=jnp.float32)
    return top, mass, total


def extend_row(state, rows, keys, values, left):
    top, mass, total = state
    scores = against(rows, keys)
    key = lax.broadcasted_iota(jnp.int32, scores.shape, 1)
    scores = jnp.where(key < left, scores, -jnp.inf)
    higher = jnp.maximum(top, jnp.max(scores, axis=1, keepdims=True))
    fade = jnp.exp2((top - higher) * EXPONENT)
    weights = jnp.exp2((scores - higher) * EXPONENT)
    mass = mass * fade + jnp.sum(weights, axis=1, keepdims=True)
    total = total * fade + jnp.dot(weights.astype(jnp.bfloat16), values, preferred_element_type=jnp.float32)
    return higher, mass, total


def close_row(state):
    _, mass, total = state
    done = total / mass
    return jnp.concatenate([done[q * STEPS : (q + 1) * STEPS] for q in range(GROUP)], axis=1).astype(
        jnp.bfloat16
    )


def resident_kernel(len_ref, table_ref, query_ref, fresh_ref, cache_ref, out_ref, arrived_ref, hold, zeros, in_sem, zero_sem):
    resident, context = cache_ref.shape[0], cache_ref.shape[1]
    tiles = context // TILE
    slots = arrived_ref.shape[0]

    def fetch(r, c):
        part = pl.ds(c * TILE, TILE)
        return pltpu.make_async_copy(cache_ref.at[r, part], hold.at[r, part], in_sem.at[r, c])

    for r in range(resident):
        for c in range(tiles):

            @pl.when(c * TILE < len_ref[0, r])
            def _():
                fetch(r, c).start()

    def clear(s):
        return pltpu.make_async_copy(zeros, arrived_ref.at[s], zero_sem.at[s])

    zeros[...] = jnp.zeros_like(zeros)
    for s in range(slots):
        clear(s).start()

    def one_row(r, carry):
        rows = query_rows(query_ref[r])
        length = jnp.where(r < resident, len_ref[0, jnp.minimum(r, resident - 1)], 0)

        def tile(c, state):
            fetch(r, c).wait()
            part = pl.ds(pl.multiple_of(c * TILE, TILE), TILE)
            keys = hold[r, part, :HEAD]
            values = hold[r, part, HEAD:]
            return extend_row(state, rows, keys, values, length - c * TILE)

        state = lax.fori_loop(0, (length + TILE - 1) // TILE, tile, open_row(rows, fresh_ref[r]))
        out_ref[r] = close_row(state)
        return carry

    lax.fori_loop(0, query_ref.shape[0], one_row, 0)
    for s in range(slots):
        clear(s).wait()


def resident(lengths, table, queries, fresh, cache, slots, positions):
    smem = pl.BlockSpec(memory_space=pltpu.SMEM)
    vmem = pl.BlockSpec(memory_space=pltpu.VMEM)
    hbm = pl.BlockSpec(memory_space=pltpu.HBM)
    rows, context = cache.shape[0], cache.shape[1]
    return pl.pallas_call(
        resident_kernel,
        out_shape=(
            jax.ShapeDtypeStruct(queries.shape, jnp.bfloat16),
            jax.ShapeDtypeStruct((slots, positions // CHUNK, CHUNK, 2 * HEAD), jnp.bfloat16),
        ),
        in_specs=[smem, smem, vmem, vmem, hbm],
        out_specs=(vmem, hbm),
        scratch_shapes=[
            pltpu.VMEM((rows, context, 2 * HEAD), jnp.bfloat16),
            pltpu.VMEM((positions // CHUNK, CHUNK, 2 * HEAD), jnp.bfloat16),
            pltpu.SemaphoreType.DMA((rows, context // TILE)),
            pltpu.SemaphoreType.DMA((slots,)),
        ],
        compiler_params=pltpu.CompilerParams(vmem_limit_bytes=VMEM),
        cost_estimate=pl.CostEstimate(flops=1 << 31, bytes_accessed=20 << 20, transcendentals=4 << 20),
        name="resident",
    )(lengths, table, queries, fresh, cache)


def slot_kernel(
    first, shared, table_ref, query_ref, fresh_ref, codes_ref, _out, _arrived, out_ref, arrived_ref,
    hold, answer, in_sem, key_sem, value_sem, answer_sem,
):
    resident = out_ref.shape[0] - query_ref.shape[0]
    tiles = codes_ref.shape[-3] // SPAN
    groups = 4

    def fetch(g, c):
        part = pl.ds(c * SPAN, SPAN)
        return pltpu.make_async_copy(codes_ref.at[g, part], hold.at[g, part], in_sem.at[g, c])

    def put(g, c):
        part = pl.ds(c * SPAN, SPAN)
        slot = table_ref[first + 4 + g]
        chunks = hold.at[0 if shared else g, part]
        target = arrived_ref.at[slot, part]
        return (
            pltpu.make_async_copy(chunks.at[:, pl.ds(0, CHUNK)], target.at[:, :, pl.ds(0, HEAD)], key_sem.at[g, c]),
            pltpu.make_async_copy(
                chunks.at[:, pl.ds(CHUNK, CHUNK)], target.at[:, :, pl.ds(HEAD, HEAD)], value_sem.at[g, c]
            ),
        )

    def reply(g):
        slot = table_ref[first + 4 + g]
        return pltpu.make_async_copy(answer.at[0 if shared else g], out_ref.at[resident + slot], answer_sem.at[g])

    def inside(codes, left):
        chunk = lax.broadcasted_iota(jnp.int32, codes.shape, 0)
        row = lax.broadcasted_iota(jnp.int32, codes.shape, 1) & (CHUNK - 1)
        return jnp.where(chunk * CHUNK + row < left, codes.astype(jnp.float32), 0.0).astype(jnp.bfloat16)

    if not shared:
        for g in range(groups):
            for c in range(tiles):

                @pl.when(c * TILE < table_ref[first + g])
                def _():
                    fetch(g, c).start()

    def scaled(codes, factors, which):
        wide = codes.astype(jnp.float32)
        rows = []
        for p in range(SPAN):
            for k in range(CHUNK // BLOCK):
                factor = factors[p, 2 * k + which : 2 * k + which + 1, :]
                rows.append(wide[p, k * BLOCK : (k + 1) * BLOCK, :] * factor)
        return jnp.concatenate(rows, axis=0).astype(jnp.bfloat16)

    def one_slot(g, carry):
        length = table_ref[first + g]
        slot = table_ref[first + 4 + g]
        at = 0 if shared else g

        @pl.when(length > 0)
        def _():
            rows = query_rows(query_ref[slot])

            def tile(c, state):
                part = pl.ds(pl.multiple_of(c * SPAN, SPAN), SPAN)
                left = length - c * TILE
                if shared:
                    hold[0, part, :FACTORS, :] = inside(codes_ref[part, :FACTORS, :], left)
                    factors = codes_ref[part, FACTORS:, :].astype(jnp.float32)
                else:
                    fetch(g, c).wait()

                    @pl.when(left < TILE)
                    def _():
                        hold[at, part, :FACTORS, :] = inside(hold[at, part, :FACTORS, :], left)

                    factors = hold[at, part, FACTORS:, :].astype(jnp.float32)
                for copy in put(g, c):
                    copy.start()
                keys = scaled(hold[at, part, :CHUNK, :], factors, 0)
                values = scaled(hold[at, part, CHUNK:FACTORS, :], factors, 1)
                return extend_row(state, rows, keys, values, left)

            state = lax.fori_loop(0, (length + TILE - 1) // TILE, tile, open_row(rows, fresh_ref[slot]))
            answer[at] = close_row(state)
            reply(g).start()

        return carry

    lax.fori_loop(0, groups, one_slot, 0)
    for g in range(groups):

        @pl.when(table_ref[first + g] > 0)
        def _():
            reply(g).wait()

        for c in range(tiles):

            @pl.when(c * TILE < table_ref[first + g])
            def _():
                for copy in put(g, c):
                    copy.wait()


def fill_slots(first, shared, table, queries, fresh, codes, out, arrived):
    smem = pl.BlockSpec(memory_space=pltpu.SMEM)
    vmem = pl.BlockSpec(memory_space=pltpu.VMEM)
    hbm = pl.BlockSpec(memory_space=pltpu.HBM)
    slots = arrived.shape[0]
    entries, chunks = 1 if shared else codes.shape[0], codes.shape[-3]
    tail = lambda width: pl.BlockSpec((slots, STEPS, width), lambda n: (1, 0, 0))
    rows = FACTORS if shared else CHUNK_ROWS
    return pl.pallas_call(
        functools.partial(slot_kernel, first, shared),
        grid=(1,),
        out_shape=(
            jax.ShapeDtypeStruct(out.shape, out.dtype),
            jax.ShapeDtypeStruct(arrived.shape, arrived.dtype),
        ),
        in_specs=[smem, tail(queries.shape[-1]), tail(2 * HEAD), vmem if shared else hbm, hbm, hbm],
        out_specs=(hbm, hbm),
        input_output_aliases={4: 0, 5: 1},
        scratch_shapes=[
            pltpu.VMEM((entries, chunks, rows, HEAD), jnp.bfloat16),
            pltpu.VMEM((entries, STEPS, queries.shape[-1]), jnp.bfloat16),
            pltpu.SemaphoreType.DMA((4, chunks // SPAN)),
            pltpu.SemaphoreType.DMA((4, chunks // SPAN)),
            pltpu.SemaphoreType.DMA((4, chunks // SPAN)),
            pltpu.SemaphoreType.DMA((4,)),
        ],
        compiler_params=pltpu.CompilerParams(vmem_limit_bytes=VMEM),
        cost_estimate=pl.CostEstimate(flops=1 << 30, bytes_accessed=8 << 20, transcendentals=1 << 20),
        name="moved_slots" if first == MOVED_LEN else "kept_slots",
    )(table, queries, fresh, codes, out, arrived)


def leave_kernel(shift, table_ref, codes_ref, out_ref, sem):
    rows = pl.ds(0, out_ref.shape[0])
    copy = pltpu.make_async_copy(codes_ref.at[table_ref[SEND + shift], rows], out_ref, sem)
    copy.start()
    copy.wait()


def leave(shift, size, table, codes):
    return pl.pallas_call(
        functools.partial(leave_kernel, shift),
        out_shape=jax.ShapeDtypeStruct((size // CHUNK,) + codes.shape[2:], codes.dtype),
        in_specs=[pl.BlockSpec(memory_space=pltpu.SMEM), pl.BlockSpec(memory_space=pl.ANY)],
        out_specs=pl.BlockSpec(memory_space=pltpu.VMEM),
        scratch_shapes=[pltpu.SemaphoreType.DMA],
        compiler_params=pltpu.CompilerParams(vmem_limit_bytes=VMEM),
        name="leave",
    )(table, codes)


def shifted(values, shift):
    return lax.ppermute(values, "src", [(g, (g + shift) % 4) for g in range(4)])


def on_device(
    prefill_pool,
    block_scales,
    block_table,
    prompt_len,
    dest_group,
    res_len,
    res_cache,
    queries,
    new_kv,
):
    everywhere = ("src", "section", "tp")
    me = lax.axis_index("src").astype(jnp.int32).reshape(1)
    layers, heads, block_len, width = prefill_pool.shape[4:]
    pool = prefill_pool.reshape(16, layers * heads, block_len, width)
    slots = queries.shape[1] - res_cache.shape[1]
    positions = 32 * 4 * block_len
    query_view, fresh_view = queries[0, :, 0], new_kv[0, :, 0]

    scales = block_scales.reshape(16, layers * heads, 1, 2).transpose(1, 2, 3, 0)
    scales = jnp.broadcast_to(scales, (layers * heads, 4, 2, 16)).reshape(layers * heads * 8, 16)
    packed, table = pack(me, dest_group.transpose(0, 2, 1), prompt_len, block_table, scales, pool)
    landed = lax.all_to_all(
        packed.reshape(128, CHUNK_ROWS, HEAD), everywhere, split_axis=0, concat_axis=0, tiled=True
    ).reshape(4, 32, CHUNK_ROWS, HEAD)
    out, arrived = resident(res_len, table, query_view, fresh_view, res_cache[0, :, 0], slots, positions)

    def kept(landed, out, arrived):
        return fill_slots(KEPT_LEN, False, table, query_view, fresh_view, landed, out, arrived)

    def moved(shared, codes, out, arrived):
        return fill_slots(MOVED_LEN, shared, table, query_view, fresh_view, codes, out, arrived)

    def general(landed, out, arrived):
        codes = jnp.zeros_like(landed)
        for shift in range(1, 4):
            hit = table[MOVED_SHIFT : MOVED_SHIFT + 4] == shift
            codes = jnp.where(hit[:, None, None, None], shifted(landed, shift), codes)
        out, arrived = kept(landed, out, arrived)
        return moved(False, codes, out, arrived)

    def direct(shift, size, landed, out, arrived):
        codes = shifted(leave(shift, size, table, landed), shift)
        out, arrived = kept(landed, out, arrived)
        return moved(True, codes, out, arrived)

    branches = [general] + [
        functools.partial(direct, shift, size) for shift in range(1, 4) for size in SIZES
    ]
    out, arrived = lax.switch(table[BRANCH], branches, landed, out, arrived)
    return out[None, :, None], arrived.reshape(slots, positions, width)[None, :, None]


def solution(mesh):
    return jax.shard_map(
        on_device,
        mesh=mesh,
        in_specs=(
            P("src", "section", "tp", None, None, None, None, None),
            P("src", "section", "tp", None, None, None, None),
            P("src", "section", "tp", None),
            P(),
            P(),
            P("src", None),
            P("section", "src", "tp", None, None),
            P("section", "src", "tp", None, None),
            P("section", "src", "tp", None, None),
        ),
        out_specs=(P("section", "src", "tp", None, None), P("section", "src", "tp", None, None)),
        check_vma=False,
    )
```

```python
import functools
import math

import jax
import jax.numpy as jnp
from jax import lax
from jax.experimental import pallas as pl
from jax.experimental.pallas import tpu as pltpu
from jax.sharding import PartitionSpec as P

HEAD = 128
STEPS = 8
GROUP = 16
QUERIES = STEPS * GROUP
TILE = 512
BLOCK = 16
CHUNK = 4 * BLOCK
SPAN = TILE // CHUNK
FACTORS = 2 * CHUNK
CHUNK_ROWS = 2 * CHUNK + 8
LEAVING = 4
EXPONENT = math.log2(math.e) / math.sqrt(HEAD)
SIZES = (512, 896, 1152, 1536, 2048)
VMEM = 66_600_000

KEPT_LEN, KEPT_SLOT = 0, 4
MOVED_LEN, MOVED_SLOT, MOVED_SHIFT = 8, 12, 16
SEND, BRANCH = 20, 24
TABLE = 32


def routes(dest, length):
    count = len(dest)
    same = [[dest[i] == dest[j] for j in range(count)] for i in range(count)]
    one = lambda flag: jnp.where(flag, 1, 0)
    moved, rank = [], []
    for i in range(count):
        flag = jnp.int32(0)
        place = jnp.int32(0)
        for j in range(count):
            if j == i:
                continue
            longer = length[j] >= length[i] if j < i else length[j] > length[i]
            flag = flag + one(jnp.logical_and(same[i][j], longer))
            if j < i:
                place = place + one(same[i][j])
        moved.append(flag > 0)
        rank.append(place)
    free = []
    for plane in range(count):
        named = jnp.int32(0)
        for i in range(count):
            named = named + one(dest[i] == plane)
        free.append(named == 0)
    planes = []
    before = jnp.int32(0)
    for i in range(count):
        choice = jnp.int32(0)
        seen = jnp.int32(0)
        for plane in range(count):
            choice = jnp.where(jnp.logical_and(free[plane], seen == before), plane, choice)
            seen = seen + one(free[plane])
        planes.append(jnp.where(moved[i], choice, dest[i]))
        before = before + one(moved[i])
    return planes, moved, rank


def fill_table(me, dest_ref, len_ref, table_ref):
    groups, requests = 4, 4
    for n in range(TABLE):
        table_ref[n] = 0
    crowded = jnp.int32(0)
    longest = jnp.int32(0)
    shifts_used = [jnp.int32(0)] * 4
    at_plane = [[jnp.int32(0)] * 4 for _ in range(4)]
    for g in range(groups):
        dest = [dest_ref[g, 0, i] for i in range(requests)]
        length = [len_ref[g, i] for i in range(requests)]
        planes, moved, rank = routes(dest, length)
        for i in range(requests):
            slot = g * 2 + rank[i]
            shift = (dest[i] - planes[i] + 4) & 3
            kept = jnp.logical_and(dest[i] == me, jnp.logical_not(moved[i]))

            @pl.when(kept)
            def _():
                table_ref[KEPT_LEN + g] = length[i]
                table_ref[KEPT_SLOT + g] = slot

            @pl.when(jnp.logical_and(moved[i], dest[i] == me))
            def _():
                table_ref[MOVED_LEN + g] = length[i]
                table_ref[MOVED_SLOT + g] = slot
                table_ref[MOVED_SHIFT + g] = shift

            @pl.when(jnp.logical_and(moved[i], planes[i] == me))
            def _():
                table_ref[SEND + shift] = g

            longest = jnp.where(moved[i], jnp.maximum(longest, length[i]), longest)
            for s in range(1, 4):
                hit = jnp.logical_and(moved[i], shift == s)
                shifts_used[s] = jnp.where(hit, 1, shifts_used[s])
                for m in range(4):
                    more = at_plane[m][s] + jnp.where(jnp.logical_and(hit, planes[i] == m), 1, 0)
                    at_plane[m][s] = more
                    crowded = jnp.where(more > 1, 1, crowded)
    kinds = shifts_used[1] + shifts_used[2] + shifts_used[3]
    which = shifts_used[2] + 2 * shifts_used[3]
    size = jnp.int32(0)
    for limit in SIZES[:-1]:
        size = size + jnp.where(longest > limit, 1, 0)
    simple = jnp.logical_and(kinds == 1, crowded == 0)
    table_ref[BRANCH] = jnp.where(simple, 1 + which * len(SIZES) + size, 0)


def pack_kernel(
    me_ref, dest_ref, len_ref, block_ref, scale_ref, pool_ref, out_ref, ready_ref,
    hold, wide, in_sem, key_sem, value_sem, wide_sem,
):
    requests = 4
    me = me_ref[0]
    ready_ref[0] = me

    def fetch(n):
        return pltpu.make_async_copy(pool_ref.at[block_ref[0, 0, 0, n]], hold.at[n], in_sem.at[n])

    for n in range(16):
        fetch(n).start()
    own_planes, _, _ = routes(
        [dest_ref[me, 0, i] for i in range(requests)],
        [len_ref[me, i] for i in range(requests)],
    )

    def place(n):
        block = (n % 4) * BLOCK
        keys = out_ref.at[own_planes[n // 4], :, pl.ds(block, BLOCK)]
        values = out_ref.at[own_planes[n // 4], :, pl.ds(CHUNK + block, BLOCK)]
        return (
            pltpu.make_async_copy(hold.at[n, :, :, pl.ds(0, HEAD)], keys, key_sem.at[n]),
            pltpu.make_async_copy(hold.at[n, :, :, pl.ds(HEAD, HEAD)], values, value_sem.at[n]),
        )

    def place_factors(i):
        rows = out_ref.at[own_planes[i], :, pl.ds(FACTORS, 8)]
        return pltpu.make_async_copy(wide.at[i], rows, wide_sem.at[i])

    pairs = scale_ref[...]
    row = lax.broadcasted_iota(jnp.int32, (4 * pairs.shape[0], pairs.shape[0]), 0)
    column = lax.broadcasted_iota(jnp.int32, row.shape, 1)
    repeat = jnp.where(column == (row >> 3) * 2 + (row & 1), 1.0, 0.0).astype(jnp.bfloat16)
    scales = jnp.dot(repeat, pairs, preferred_element_type=jnp.float32)
    block = (lax.broadcasted_iota(jnp.int32, scales.shape, 0) >> 1) & 3
    entry = lax.broadcasted_iota(jnp.int32, scales.shape, 1)
    ones = jnp.ones((scales.shape[1], HEAD), jnp.bfloat16)
    for i in range(requests):
        wanted = jnp.full(scales.shape, block_ref[0, 0, 0, 4 * i], jnp.int32)
        for k in range(1, 4):
            wanted = jnp.where(block == k, block_ref[0, 0, 0, 4 * i + k], wanted)
        picked = jnp.where(entry == wanted, scales, 0.0).astype(jnp.bfloat16)
        spread = jnp.dot(picked, ones, preferred_element_type=jnp.float32)
        wide[i] = spread.reshape(wide.shape[1:]).astype(jnp.bfloat16)
        place_factors(i).start()

    for n in range(16):
        fetch(n).wait()
        for copy in place(n):
            copy.start()

    for n in range(16):
        for copy in place(n):
            copy.wait()
    for i in range(requests):
        place_factors(i).wait()


def pack(me, dest, lengths, blocks, scales, pool):
    smem = pl.BlockSpec(memory_space=pltpu.SMEM)
    vmem = pl.BlockSpec(memory_space=pltpu.VMEM)
    hbm = pl.BlockSpec(memory_space=pltpu.HBM)
    return pl.pallas_call(
        pack_kernel,
        out_shape=(
            jax.ShapeDtypeStruct((4, 32, CHUNK_ROWS, HEAD), jnp.bfloat16),
            jax.ShapeDtypeStruct((1,), jnp.int32),
        ),
        in_specs=[smem, smem, smem, smem, vmem, hbm],
        out_specs=(hbm, smem),
        scratch_shapes=[
            pltpu.VMEM((16, 32, BLOCK, 2 * HEAD), jnp.bfloat16),
            pltpu.VMEM((4, 32, 8, HEAD), jnp.bfloat16),
            pltpu.SemaphoreType.DMA((16,)),
            pltpu.SemaphoreType.DMA((16,)),
            pltpu.SemaphoreType.DMA((16,)),
            pltpu.SemaphoreType.DMA((4,)),
        ],
        compiler_params=pltpu.CompilerParams(vmem_limit_bytes=VMEM),
        cost_estimate=pl.CostEstimate(flops=0, bytes_accessed=8 << 20, transcendentals=0),
        name="pack",
    )(me, dest, lengths, blocks, scales, pool)


def query_rows(query):
    wide = query.astype(jnp.float32)
    return jnp.concatenate([wide[:, q * HEAD : (q + 1) * HEAD] for q in range(GROUP)], axis=0).astype(
        jnp.bfloat16
    )


def against(rows, keys):
    return lax.dot_general(rows, keys, (((1,), (1,)), ((), ())), preferred_element_type=jnp.float32)


def open_row(rows, fresh):
    scores = against(rows, fresh[:, :HEAD])
    step = lax.broadcasted_iota(jnp.int32, scores.shape, 0) & (STEPS - 1)
    key = lax.broadcasted_iota(jnp.int32, scores.shape, 1)
    scores = jnp.where(key <= step, scores, -jnp.inf)
    top = jnp.max(scores, axis=1, keepdims=True)
    weights = jnp.exp2((scores - top) * EXPONENT)
    mass = jnp.sum(weights, axis=1, keepdims=True)
    total = jnp.dot(weights.astype(jnp.bfloat16), fresh[:, HEAD:], preferred_element_type=jnp.float32)
    return top, mass, total


def extend_row(state, rows, keys, values, left):
    top, mass, total = state
    scores = against(rows, keys)
    key = lax.broadcasted_iota(jnp.int32, scores.shape, 1)
    scores = jnp.where(key < left, scores, -jnp.inf)
    higher = jnp.maximum(top, jnp.max(scores, axis=1, keepdims=True))
    fade = jnp.exp2((top - higher) * EXPONENT)
    weights = jnp.exp2((scores - higher) * EXPONENT)
    mass = mass * fade + jnp.sum(weights, axis=1, keepdims=True)
    total = total * fade + jnp.dot(weights.astype(jnp.bfloat16), values, preferred_element_type=jnp.float32)
    return higher, mass, total


def close_row(state):
    _, mass, total = state
    done = total / mass
    return jnp.concatenate([done[q * STEPS : (q + 1) * STEPS] for q in range(GROUP)], axis=1).astype(
        jnp.bfloat16
    )


def resident_kernel(
    ready_ref, dest_ref, prompt_ref, len_ref, query_ref, fresh_ref, cache_ref, out_ref, arrived_ref, table_ref,
    hold, zeros, in_sem, zero_sem,
):
    resident, context = cache_ref.shape[0], cache_ref.shape[1]
    tiles = context // TILE
    slots = arrived_ref.shape[0]

    def fetch(r, c):
        part = pl.ds(c * TILE, TILE)
        return pltpu.make_async_copy(cache_ref.at[r, part], hold.at[r, part], in_sem.at[r, c])

    for r in range(resident):
        for c in range(tiles):

            @pl.when(c * TILE < len_ref[0, r])
            def _():
                fetch(r, c).start()

    def clear(s):
        return pltpu.make_async_copy(zeros, arrived_ref.at[s], zero_sem.at[s])

    zeros[...] = jnp.zeros_like(zeros)
    for s in range(slots):
        clear(s).start()
    fill_table(ready_ref[0], dest_ref, prompt_ref, table_ref)

    def one_row(r, carry):
        rows = query_rows(query_ref[r])
        length = jnp.where(r < resident, len_ref[0, jnp.minimum(r, resident - 1)], 0)

        def tile(c, state):
            fetch(r, c).wait()
            part = pl.ds(pl.multiple_of(c * TILE, TILE), TILE)
            keys = hold[r, part, :HEAD]
            values = hold[r, part, HEAD:]
            return extend_row(state, rows, keys, values, length - c * TILE)

        state = lax.fori_loop(0, (length + TILE - 1) // TILE, tile, open_row(rows, fresh_ref[r]))
        out_ref[r] = close_row(state)
        return carry

    lax.fori_loop(0, query_ref.shape[0], one_row, 0)
    for s in range(slots):
        clear(s).wait()


def resident(ready, dest, prompts, lengths, queries, fresh, cache, slots, positions):
    smem = pl.BlockSpec(memory_space=pltpu.SMEM)
    vmem = pl.BlockSpec(memory_space=pltpu.VMEM)
    hbm = pl.BlockSpec(memory_space=pltpu.HBM)
    rows, context = cache.shape[0], cache.shape[1]
    return pl.pallas_call(
        resident_kernel,
        out_shape=(
            jax.ShapeDtypeStruct(queries.shape, jnp.bfloat16),
            jax.ShapeDtypeStruct((slots, positions // CHUNK, CHUNK, 2 * HEAD), jnp.bfloat16),
            jax.ShapeDtypeStruct((TABLE,), jnp.int32),
        ),
        in_specs=[smem, smem, smem, smem, vmem, vmem, hbm],
        out_specs=(vmem, hbm, smem),
        scratch_shapes=[
            pltpu.VMEM((rows, context, 2 * HEAD), jnp.bfloat16),
            pltpu.VMEM((positions // CHUNK, CHUNK, 2 * HEAD), jnp.bfloat16),
            pltpu.SemaphoreType.DMA((rows, context // TILE)),
            pltpu.SemaphoreType.DMA((slots,)),
        ],
        compiler_params=pltpu.CompilerParams(vmem_limit_bytes=VMEM),
        cost_estimate=pl.CostEstimate(flops=1 << 31, bytes_accessed=20 << 20, transcendentals=4 << 20),
        name="resident",
    )(ready, dest, prompts, lengths, queries, fresh, cache)


def slot_kernel(
    first, shared, table_ref, query_ref, fresh_ref, codes_ref, _out, _arrived, out_ref, arrived_ref,
    hold, answer, in_sem, key_sem, value_sem, answer_sem,
):
    resident = out_ref.shape[0] - query_ref.shape[0]
    chunks = codes_ref.shape[-3]
    tiles = pl.cdiv(chunks, SPAN)
    groups = 4

    def fetch(g, c, count=None):
        part = pl.ds(c * SPAN, count or min(SPAN, chunks - c * SPAN))
        if shared:
            return pltpu.make_async_copy(codes_ref.at[part], hold.at[0, part], in_sem.at[g, c])
        return pltpu.make_async_copy(codes_ref.at[g, part], hold.at[g, part], in_sem.at[g, c])

    def put(g, c):
        part = pl.ds(c * SPAN, SPAN)
        slot = table_ref[first + 4 + g]
        chunks = hold.at[0 if shared else g, part]
        target = arrived_ref.at[slot, part]
        return (
            pltpu.make_async_copy(chunks.at[:, pl.ds(0, CHUNK)], target.at[:, :, pl.ds(0, HEAD)], key_sem.at[g, c]),
            pltpu.make_async_copy(
                chunks.at[:, pl.ds(CHUNK, CHUNK)], target.at[:, :, pl.ds(HEAD, HEAD)], value_sem.at[g, c]
            ),
        )

    def reply(g):
        slot = table_ref[first + 4 + g]
        return pltpu.make_async_copy(answer.at[0 if shared else g], out_ref.at[resident + slot], answer_sem.at[g])

    def inside(codes, left):
        chunk = lax.broadcasted_iota(jnp.int32, codes.shape, 0)
        row = lax.broadcasted_iota(jnp.int32, codes.shape, 1) & (CHUNK - 1)
        return jnp.where(chunk * CHUNK + row < left, codes.astype(jnp.float32), 0.0).astype(jnp.bfloat16)

    if chunks < tiles * SPAN:
        rest = pl.ds(chunks, tiles * SPAN - chunks)
        hold[0, rest, :, :] = jnp.zeros_like(hold[0, rest, :, :])
    for g in range(groups):
        for c in range(tiles):

            @pl.when(c * TILE < table_ref[first + g])
            def _():
                fetch(g, c).start()

    def scaled(codes, factors, which):
        wide = codes.astype(jnp.float32)
        rows = []
        for p in range(SPAN):
            for k in range(CHUNK // BLOCK):
                factor = factors[p, 2 * k + which : 2 * k + which + 1, :]
                rows.append(wide[p, k * BLOCK : (k + 1) * BLOCK, :] * factor)
        return jnp.concatenate(rows, axis=0).astype(jnp.bfloat16)

    def one_slot(g, carry):
        length = table_ref[first + g]
        slot = table_ref[first + 4 + g]
        at = 0 if shared else g

        @pl.when(length > 0)
        def _():
            rows = query_rows(query_ref[slot])

            def tile(c, state):
                part = pl.ds(pl.multiple_of(c * SPAN, SPAN), SPAN)
                left = length - c * TILE
                if chunks == tiles * SPAN:
                    fetch(g, c, SPAN).wait()
                else:

                    @pl.when(c < tiles - 1)
                    def _():
                        fetch(g, c, SPAN).wait()

                    @pl.when(c == tiles - 1)
                    def _():
                        fetch(g, tiles - 1).wait()

                @pl.when(left < TILE)
                def _():
                    hold[at, part, :FACTORS, :] = inside(hold[at, part, :FACTORS, :], left)

                factors = hold[at, part, FACTORS:, :].astype(jnp.float32)
                for copy in put(g, c):
                    copy.start()
                keys = scaled(hold[at, part, :CHUNK, :], factors, 0)
                values = scaled(hold[at, part, CHUNK:FACTORS, :], factors, 1)
                return extend_row(state, rows, keys, values, left)

            state = lax.fori_loop(0, (length + TILE - 1) // TILE, tile, open_row(rows, fresh_ref[slot]))
            answer[at] = close_row(state)
            reply(g).start()

        return carry

    lax.fori_loop(0, groups, one_slot, 0)
    for g in range(groups):

        @pl.when(table_ref[first + g] > 0)
        def _():
            reply(g).wait()

        for c in range(tiles):

            @pl.when(c * TILE < table_ref[first + g])
            def _():
                for copy in put(g, c):
                    copy.wait()


def fill_slots(first, shared, table, queries, fresh, codes, out, arrived):
    smem = pl.BlockSpec(memory_space=pltpu.SMEM)
    vmem = pl.BlockSpec(memory_space=pltpu.VMEM)
    hbm = pl.BlockSpec(memory_space=pltpu.HBM)
    slots = arrived.shape[0]
    entries, tiles = 1 if shared else codes.shape[0], pl.cdiv(codes.shape[-3], SPAN)
    tail = lambda width: pl.BlockSpec((slots, STEPS, width), lambda n: (1, 0, 0))
    return pl.pallas_call(
        functools.partial(slot_kernel, first, shared),
        grid=(1,),
        out_shape=(
            jax.ShapeDtypeStruct(out.shape, out.dtype),
            jax.ShapeDtypeStruct(arrived.shape, arrived.dtype),
        ),
        in_specs=[smem, tail(queries.shape[-1]), tail(2 * HEAD), hbm, hbm, hbm],
        out_specs=(hbm, hbm),
        input_output_aliases={4: 0, 5: 1},
        scratch_shapes=[
            pltpu.VMEM((entries, tiles * SPAN, CHUNK_ROWS, HEAD), jnp.bfloat16),
            pltpu.VMEM((entries, STEPS, queries.shape[-1]), jnp.bfloat16),
            pltpu.SemaphoreType.DMA((4, tiles)),
            pltpu.SemaphoreType.DMA((4, tiles)),
            pltpu.SemaphoreType.DMA((4, tiles)),
            pltpu.SemaphoreType.DMA((4,)),
        ],
        compiler_params=pltpu.CompilerParams(vmem_limit_bytes=VMEM),
        cost_estimate=pl.CostEstimate(flops=1 << 30, bytes_accessed=8 << 20, transcendentals=1 << 20),
        name="moved_slots" if first == MOVED_LEN else "kept_slots",
    )(table, queries, fresh, codes, out, arrived)


def leave_kernel(shift, table_ref, codes_ref, out_ref, hold, in_sem, out_sem):
    chunks = out_ref.shape[0]
    parts = [pl.ds(start, min(LEAVING, chunks - start)) for start in range(0, chunks, LEAVING)]
    group = table_ref[SEND + shift]

    def fetch(n):
        return pltpu.make_async_copy(codes_ref.at[group, parts[n]], hold.at[parts[n]], in_sem.at[n])

    def place(n):
        return pltpu.make_async_copy(hold.at[parts[n]], out_ref.at[parts[n]], out_sem.at[n])

    for n in range(len(parts)):
        fetch(n).start()
    for n in range(len(parts)):
        fetch(n).wait()
        place(n).start()
    for n in range(len(parts)):
        place(n).wait()


def leave(shift, size, table, codes):
    hbm = pl.BlockSpec(memory_space=pltpu.HBM)
    shape = (size // CHUNK,) + codes.shape[2:]
    copies = pl.cdiv(shape[0], LEAVING)
    return pl.pallas_call(
        functools.partial(leave_kernel, shift),
        out_shape=jax.ShapeDtypeStruct(shape, codes.dtype),
        in_specs=[pl.BlockSpec(memory_space=pltpu.SMEM), hbm],
        out_specs=hbm,
        scratch_shapes=[
            pltpu.VMEM(shape, codes.dtype),
            pltpu.SemaphoreType.DMA((copies,)),
            pltpu.SemaphoreType.DMA((copies,)),
        ],
        compiler_params=pltpu.CompilerParams(vmem_limit_bytes=VMEM),
        name="leave",
    )(table, codes)


def shifted(values, shift):
    return lax.ppermute(values, "src", [(g, (g + shift) % 4) for g in range(4)])


def on_device(
    prefill_pool,
    block_scales,
    block_table,
    prompt_len,
    dest_group,
    res_len,
    res_cache,
    queries,
    new_kv,
):
    everywhere = ("src", "section", "tp")
    me = lax.axis_index("src").astype(jnp.int32).reshape(1)
    layers, heads, block_len, width = prefill_pool.shape[4:]
    pool = prefill_pool.reshape(16, layers * heads, block_len, width)
    slots = queries.shape[1] - res_cache.shape[1]
    positions = 32 * 4 * block_len
    query_view, fresh_view = queries[0, :, 0], new_kv[0, :, 0]

    scales = block_scales.reshape(16, layers * heads, 2).transpose(1, 2, 0).reshape(layers * heads * 2, 16)
    dest = dest_group.transpose(0, 2, 1)
    packed, ready = pack(me, dest, prompt_len, block_table, scales, pool)
    landed = lax.all_to_all(
        packed.reshape(128, CHUNK_ROWS, HEAD), everywhere, split_axis=0, concat_axis=0, tiled=True
    ).reshape(4, 32, CHUNK_ROWS, HEAD)
    out, arrived, table = resident(
        ready, dest, prompt_len, res_len, query_view, fresh_view, res_cache[0, :, 0], slots, positions
    )

    def kept(landed, out, arrived):
        return fill_slots(KEPT_LEN, False, table, query_view, fresh_view, landed, out, arrived)

    def moved(shared, codes, out, arrived):
        return fill_slots(MOVED_LEN, shared, table, query_view, fresh_view, codes, out, arrived)

    def general(landed, out, arrived):
        codes = jnp.zeros_like(landed)
        for shift in range(1, 4):
            hit = table[MOVED_SHIFT : MOVED_SHIFT + 4] == shift
            codes = jnp.where(hit[:, None, None, None], shifted(landed, shift), codes)
        out, arrived = kept(landed, out, arrived)
        return moved(False, codes, out, arrived)

    def direct(shift, size, landed, out, arrived):
        codes = shifted(leave(shift, size, table, landed), shift)
        out, arrived = kept(landed, out, arrived)
        return moved(True, codes, out, arrived)

    branches = [general] + [
        functools.partial(direct, shift, size) for shift in range(1, 4) for size in SIZES
    ]
    out, arrived = lax.switch(table[BRANCH], branches, landed, out, arrived)
    return out[None, :, None], arrived.reshape(slots, positions, width)[None, :, None]


def solution(mesh):
    return jax.shard_map(
        on_device,
        mesh=mesh,
        in_specs=(
            P("src", "section", "tp", None, None, None, None, None),
            P("src", "section", "tp", None, None, None, None),
            P("src", "section", "tp", None),
            P(),
            P(),
            P("src", None),
            P("section", "src", "tp", None, None),
            P("section", "src", "tp", None, None),
            P("section", "src", "tp", None, None),
        ),
        out_specs=(P("section", "src", "tp", None, None), P("section", "src", "tp", None, None)),
        check_vma=False,
    )
```

```python
import functools
import math

import jax
import jax.numpy as jnp
from jax import lax
from jax.experimental import pallas as pl
from jax.experimental.pallas import tpu as pltpu
from jax.sharding import PartitionSpec as P

HEAD = 128
STEPS = 8
GROUP = 16
QUERIES = STEPS * GROUP
TILE = 512
BLOCK = 16
CHUNK = 4 * BLOCK
SPAN = TILE // CHUNK
FACTORS = 2 * CHUNK
CHUNK_ROWS = 2 * CHUNK + 8
LEAVING = 4
EXPONENT = math.log2(math.e) / math.sqrt(HEAD)
SIZES = (512, 896, 1280, 2048)
VMEM = 66_950_000

KEPT_LEN, KEPT_SLOT = 0, 4
MOVED_LEN, MOVED_SLOT, MOVED_SHIFT = 8, 12, 16
SEND, BRANCH = 20, 24
TABLE = 32


def routes(dest, length):
    count = len(dest)
    same = [[dest[i] == dest[j] for j in range(count)] for i in range(count)]
    one = lambda flag: jnp.where(flag, 1, 0)
    moved, rank = [], []
    for i in range(count):
        flag = jnp.int32(0)
        place = jnp.int32(0)
        for j in range(count):
            if j == i:
                continue
            longer = length[j] >= length[i] if j < i else length[j] > length[i]
            flag = flag + one(jnp.logical_and(same[i][j], longer))
            if j < i:
                place = place + one(same[i][j])
        moved.append(flag > 0)
        rank.append(place)
    free = []
    for plane in range(count):
        named = jnp.int32(0)
        for i in range(count):
            named = named + one(dest[i] == plane)
        free.append(named == 0)
    planes = []
    before = jnp.int32(0)
    for i in range(count):
        choice = jnp.int32(0)
        seen = jnp.int32(0)
        for plane in range(count):
            choice = jnp.where(jnp.logical_and(free[plane], seen == before), plane, choice)
            seen = seen + one(free[plane])
        planes.append(jnp.where(moved[i], choice, dest[i]))
        before = before + one(moved[i])
    return planes, moved, rank


def fill_table(me, dest_ref, len_ref, table_ref):
    groups, requests = 4, 4
    for n in range(TABLE):
        table_ref[n] = 0
    crowded = jnp.int32(0)
    longest = jnp.int32(0)
    shifts_used = [jnp.int32(0)] * 4
    at_plane = [[jnp.int32(0)] * 4 for _ in range(4)]
    for g in range(groups):
        dest = [dest_ref[g, 0, i] for i in range(requests)]
        length = [len_ref[g, i] for i in range(requests)]
        planes, moved, rank = routes(dest, length)
        for i in range(requests):
            slot = g * 2 + rank[i]
            shift = (dest[i] - planes[i] + 4) & 3
            kept = jnp.logical_and(dest[i] == me, jnp.logical_not(moved[i]))

            @pl.when(kept)
            def _():
                table_ref[KEPT_LEN + g] = length[i]
                table_ref[KEPT_SLOT + g] = slot

            @pl.when(jnp.logical_and(moved[i], dest[i] == me))
            def _():
                table_ref[MOVED_LEN + g] = length[i]
                table_ref[MOVED_SLOT + g] = slot
                table_ref[MOVED_SHIFT + g] = shift

            @pl.when(jnp.logical_and(moved[i], planes[i] == me))
            def _():
                table_ref[SEND + shift] = g

            longest = jnp.where(moved[i], jnp.maximum(longest, length[i]), longest)
            for s in range(1, 4):
                hit = jnp.logical_and(moved[i], shift == s)
                shifts_used[s] = jnp.where(hit, 1, shifts_used[s])
                for m in range(4):
                    more = at_plane[m][s] + jnp.where(jnp.logical_and(hit, planes[i] == m), 1, 0)
                    at_plane[m][s] = more
                    crowded = jnp.where(more > 1, 1, crowded)
    kinds = shifts_used[1] + shifts_used[2] + shifts_used[3]
    which = shifts_used[2] + 2 * shifts_used[3]
    size = jnp.int32(0)
    for limit in SIZES[:-1]:
        size = size + jnp.where(longest > limit, 1, 0)
    simple = jnp.logical_and(kinds == 1, crowded == 0)
    table_ref[BRANCH] = jnp.where(simple, 1 + which * len(SIZES) + size, 0)


def pack_kernel(
    me_ref, dest_ref, len_ref, block_ref, scale_ref, pool_ref, out_ref, ready_ref,
    hold, wide, in_sem, key_sem, value_sem, wide_sem,
):
    requests = 4
    me = me_ref[0]
    ready_ref[0] = me

    def fetch(n):
        rows = pl.ds((n % 4) * BLOCK, BLOCK)
        return pltpu.make_async_copy(pool_ref.at[block_ref[0, 0, 0, n]], hold.at[n // 4, :, rows], in_sem.at[n])

    for n in range(16):
        fetch(n).start()
    own_planes, _, _ = routes(
        [dest_ref[me, 0, i] for i in range(requests)],
        [len_ref[me, i] for i in range(requests)],
    )

    def place(i):
        rows = out_ref.at[own_planes[i]]
        keys = hold.at[i, :, :, pl.ds(0, HEAD)]
        values = hold.at[i, :, :, pl.ds(HEAD, HEAD)]
        return (
            pltpu.make_async_copy(keys, rows.at[:, pl.ds(0, CHUNK)], key_sem.at[i]),
            pltpu.make_async_copy(values, rows.at[:, pl.ds(CHUNK, CHUNK)], value_sem.at[i]),
        )

    def place_factors(i):
        rows = out_ref.at[own_planes[i], :, pl.ds(FACTORS, 8)]
        return pltpu.make_async_copy(wide.at[i], rows, wide_sem.at[i])

    pairs = scale_ref[...]
    row = lax.broadcasted_iota(jnp.int32, (4 * pairs.shape[0], pairs.shape[0]), 0)
    column = lax.broadcasted_iota(jnp.int32, row.shape, 1)
    repeat = jnp.where(column == (row >> 3) * 2 + (row & 1), 1.0, 0.0).astype(jnp.bfloat16)
    scales = jnp.dot(repeat, pairs, preferred_element_type=jnp.float32)
    block = (lax.broadcasted_iota(jnp.int32, scales.shape, 0) >> 1) & 3
    entry = lax.broadcasted_iota(jnp.int32, scales.shape, 1)
    ones = jnp.ones((scales.shape[1], HEAD), jnp.bfloat16)
    for i in range(requests):
        wanted = jnp.full(scales.shape, block_ref[0, 0, 0, 4 * i], jnp.int32)
        for k in range(1, 4):
            wanted = jnp.where(block == k, block_ref[0, 0, 0, 4 * i + k], wanted)
        picked = jnp.where(entry == wanted, scales, 0.0).astype(jnp.bfloat16)
        spread = jnp.dot(picked, ones, preferred_element_type=jnp.float32)
        wide[i] = spread.reshape(wide.shape[1:]).astype(jnp.bfloat16)
        place_factors(i).start()

    for i in range(requests):
        for k in range(4):
            fetch(4 * i + k).wait()
        for copy in place(i):
            copy.start()

    for i in range(requests):
        for copy in place(i):
            copy.wait()
        place_factors(i).wait()


def pack(me, dest, lengths, blocks, scales, pool):
    smem = pl.BlockSpec(memory_space=pltpu.SMEM)
    vmem = pl.BlockSpec(memory_space=pltpu.VMEM)
    hbm = pl.BlockSpec(memory_space=pltpu.HBM)
    return pl.pallas_call(
        pack_kernel,
        out_shape=(
            jax.ShapeDtypeStruct((4, 32, CHUNK_ROWS, HEAD), jnp.bfloat16),
            jax.ShapeDtypeStruct((1,), jnp.int32),
        ),
        in_specs=[smem, smem, smem, smem, vmem, hbm],
        out_specs=(hbm, smem),
        scratch_shapes=[
            pltpu.VMEM((4, 32, CHUNK, 2 * HEAD), jnp.bfloat16),
            pltpu.VMEM((4, 32, 8, HEAD), jnp.bfloat16),
            pltpu.SemaphoreType.DMA((16,)),
            pltpu.SemaphoreType.DMA((4,)),
            pltpu.SemaphoreType.DMA((4,)),
            pltpu.SemaphoreType.DMA((4,)),
        ],
        compiler_params=pltpu.CompilerParams(vmem_limit_bytes=VMEM),
        cost_estimate=pl.CostEstimate(flops=0, bytes_accessed=8 << 20, transcendentals=0),
        name="pack",
    )(me, dest, lengths, blocks, scales, pool)


def query_rows(query):
    wide = query.astype(jnp.float32)
    return jnp.concatenate([wide[:, q * HEAD : (q + 1) * HEAD] for q in range(GROUP)], axis=0).astype(
        jnp.bfloat16
    )


def against(rows, keys):
    return lax.dot_general(rows, keys, (((1,), (1,)), ((), ())), preferred_element_type=jnp.float32)


def open_row(rows, fresh):
    scores = against(rows, fresh[:, :HEAD])
    step = lax.broadcasted_iota(jnp.int32, scores.shape, 0) & (STEPS - 1)
    key = lax.broadcasted_iota(jnp.int32, scores.shape, 1)
    scores = jnp.where(key <= step, scores, -jnp.inf)
    top = jnp.max(scores, axis=1, keepdims=True)
    weights = jnp.exp2((scores - top) * EXPONENT)
    mass = jnp.sum(weights, axis=1, keepdims=True)
    total = jnp.dot(weights.astype(jnp.bfloat16), fresh[:, HEAD:], preferred_element_type=jnp.float32)
    return top, mass, total


def extend_row(state, rows, keys, values, left):
    top, mass, total = state
    scores = against(rows, keys)
    key = lax.broadcasted_iota(jnp.int32, scores.shape, 1)
    scores = jnp.where(key < left, scores, -jnp.inf)
    higher = jnp.maximum(top, jnp.max(scores, axis=1, keepdims=True))
    fade = jnp.exp2((top - higher) * EXPONENT)
    weights = jnp.exp2((scores - higher) * EXPONENT)
    mass = mass * fade + jnp.sum(weights, axis=1, keepdims=True)
    total = total * fade + jnp.dot(weights.astype(jnp.bfloat16), values, preferred_element_type=jnp.float32)
    return higher, mass, total


def close_row(state):
    _, mass, total = state
    done = total / mass
    return jnp.concatenate([done[q * STEPS : (q + 1) * STEPS] for q in range(GROUP)], axis=1).astype(
        jnp.bfloat16
    )


def resident_kernel(
    ready_ref, dest_ref, prompt_ref, len_ref, query_ref, fresh_ref, cache_ref, out_ref, arrived_ref, table_ref,
    hold, zeros, in_sem, zero_sem,
):
    resident, context = cache_ref.shape[0], cache_ref.shape[1]
    tiles = context // TILE
    slots = arrived_ref.shape[0]

    def fetch(r, c):
        part = pl.ds(c * TILE, TILE)
        return pltpu.make_async_copy(cache_ref.at[r, part], hold.at[r, part], in_sem.at[r, c])

    for r in range(resident):
        for c in range(tiles):

            @pl.when(c * TILE < len_ref[0, r])
            def _():
                fetch(r, c).start()

    def clear(s):
        return pltpu.make_async_copy(zeros, arrived_ref.at[s], zero_sem.at[s])

    zeros[...] = jnp.zeros_like(zeros)
    for s in range(slots):
        clear(s).start()
    fill_table(ready_ref[0], dest_ref, prompt_ref, table_ref)

    def one_row(r, carry):
        rows = query_rows(query_ref[r])
        length = jnp.where(r < resident, len_ref[0, jnp.minimum(r, resident - 1)], 0)

        def tile(c, state):
            fetch(r, c).wait()
            part = pl.ds(pl.multiple_of(c * TILE, TILE), TILE)
            keys = hold[r, part, :HEAD]
            values = hold[r, part, HEAD:]
            return extend_row(state, rows, keys, values, length - c * TILE)

        state = lax.fori_loop(0, (length + TILE - 1) // TILE, tile, open_row(rows, fresh_ref[r]))
        out_ref[r] = close_row(state)
        return carry

    lax.fori_loop(0, query_ref.shape[0], one_row, 0)
    for s in range(slots):
        clear(s).wait()


def resident(ready, dest, prompts, lengths, queries, fresh, cache, slots, positions):
    smem = pl.BlockSpec(memory_space=pltpu.SMEM)
    vmem = pl.BlockSpec(memory_space=pltpu.VMEM)
    hbm = pl.BlockSpec(memory_space=pltpu.HBM)
    rows, context = cache.shape[0], cache.shape[1]
    return pl.pallas_call(
        resident_kernel,
        out_shape=(
            jax.ShapeDtypeStruct(queries.shape, jnp.bfloat16),
            jax.ShapeDtypeStruct((slots, positions // CHUNK, CHUNK, 2 * HEAD), jnp.bfloat16),
            jax.ShapeDtypeStruct((TABLE,), jnp.int32),
        ),
        in_specs=[smem, smem, smem, smem, vmem, vmem, hbm],
        out_specs=(vmem, hbm, smem),
        scratch_shapes=[
            pltpu.VMEM((rows, context, 2 * HEAD), jnp.bfloat16),
            pltpu.VMEM((positions // CHUNK, CHUNK, 2 * HEAD), jnp.bfloat16),
            pltpu.SemaphoreType.DMA((rows, context // TILE)),
            pltpu.SemaphoreType.DMA((slots,)),
        ],
        compiler_params=pltpu.CompilerParams(vmem_limit_bytes=VMEM),
        cost_estimate=pl.CostEstimate(flops=1 << 31, bytes_accessed=20 << 20, transcendentals=4 << 20),
        name="resident",
    )(ready, dest, prompts, lengths, queries, fresh, cache)


def slot_kernel(
    first, shared, table_ref, query_ref, fresh_ref, codes_ref, _out, _arrived, out_ref, arrived_ref,
    hold, answer, in_sem, key_sem, value_sem, answer_sem,
):
    resident = out_ref.shape[0] - query_ref.shape[0]
    chunks = codes_ref.shape[-3]
    tiles = pl.cdiv(chunks, SPAN)
    groups = 4

    def fetch(g, c, count=None):
        part = pl.ds(c * SPAN, count or min(SPAN, chunks - c * SPAN))
        if shared:
            return pltpu.make_async_copy(codes_ref.at[part], hold.at[0, part], in_sem.at[g, c])
        return pltpu.make_async_copy(codes_ref.at[g, part], hold.at[g, part], in_sem.at[g, c])

    def put(g, c):
        part = pl.ds(c * SPAN, SPAN)
        slot = table_ref[first + 4 + g]
        chunks = hold.at[0 if shared else g, part]
        target = arrived_ref.at[slot, part]
        return (
            pltpu.make_async_copy(chunks.at[:, pl.ds(0, CHUNK)], target.at[:, :, pl.ds(0, HEAD)], key_sem.at[g, c]),
            pltpu.make_async_copy(
                chunks.at[:, pl.ds(CHUNK, CHUNK)], target.at[:, :, pl.ds(HEAD, HEAD)], value_sem.at[g, c]
            ),
        )

    def reply(g):
        slot = table_ref[first + 4 + g]
        return pltpu.make_async_copy(answer.at[0 if shared else g], out_ref.at[resident + slot], answer_sem.at[g])

    def inside(codes, left):
        chunk = lax.broadcasted_iota(jnp.int32, codes.shape, 0)
        row = lax.broadcasted_iota(jnp.int32, codes.shape, 1) & (CHUNK - 1)
        return jnp.where(chunk * CHUNK + row < left, codes.astype(jnp.float32), 0.0).astype(jnp.bfloat16)

    if chunks < tiles * SPAN:
        rest = pl.ds(chunks, tiles * SPAN - chunks)
        hold[0, rest, :, :] = jnp.zeros_like(hold[0, rest, :, :])
    for g in range(groups):
        for c in range(tiles):

            @pl.when(c * TILE < table_ref[first + g])
            def _():
                fetch(g, c).start()

    def scaled(codes, factors, which):
        wide = codes.astype(jnp.float32)
        rows = []
        for p in range(SPAN):
            for k in range(CHUNK // BLOCK):
                factor = factors[p, 2 * k + which : 2 * k + which + 1, :]
                rows.append(wide[p, k * BLOCK : (k + 1) * BLOCK, :] * factor)
        return jnp.concatenate(rows, axis=0).astype(jnp.bfloat16)

    def one_slot(g, carry):
        length = table_ref[first + g]
        slot = table_ref[first + 4 + g]
        at = 0 if shared else g

        @pl.when(length > 0)
        def _():
            rows = query_rows(query_ref[slot])

            def tile(c, state):
                part = pl.ds(pl.multiple_of(c * SPAN, SPAN), SPAN)
                left = length - c * TILE
                if chunks == tiles * SPAN:
                    fetch(g, c, SPAN).wait()
                else:

                    @pl.when(c < tiles - 1)
                    def _():
                        fetch(g, c, SPAN).wait()

                    @pl.when(c == tiles - 1)
                    def _():
                        fetch(g, tiles - 1).wait()

                @pl.when(left < TILE)
                def _():
                    hold[at, part, :FACTORS, :] = inside(hold[at, part, :FACTORS, :], left)

                factors = hold[at, part, FACTORS:, :].astype(jnp.float32)
                for copy in put(g, c):
                    copy.start()
                keys = scaled(hold[at, part, :CHUNK, :], factors, 0)
                values = scaled(hold[at, part, CHUNK:FACTORS, :], factors, 1)
                return extend_row(state, rows, keys, values, left)

            state = lax.fori_loop(0, (length + TILE - 1) // TILE, tile, open_row(rows, fresh_ref[slot]))
            answer[at] = close_row(state)
            reply(g).start()

        return carry

    lax.fori_loop(0, groups, one_slot, 0)
    for g in range(groups):

        @pl.when(table_ref[first + g] > 0)
        def _():
            reply(g).wait()

        for c in range(tiles):

            @pl.when(c * TILE < table_ref[first + g])
            def _():
                for copy in put(g, c):
                    copy.wait()


def fill_slots(first, shared, table, queries, fresh, codes, out, arrived):
    smem = pl.BlockSpec(memory_space=pltpu.SMEM)
    vmem = pl.BlockSpec(memory_space=pltpu.VMEM)
    hbm = pl.BlockSpec(memory_space=pltpu.HBM)
    slots = arrived.shape[0]
    entries, tiles = 1 if shared else codes.shape[0], pl.cdiv(codes.shape[-3], SPAN)
    tail = lambda width: pl.BlockSpec((slots, STEPS, width), lambda n: (1, 0, 0))
    return pl.pallas_call(
        functools.partial(slot_kernel, first, shared),
        grid=(1,),
        out_shape=(
            jax.ShapeDtypeStruct(out.shape, out.dtype),
            jax.ShapeDtypeStruct(arrived.shape, arrived.dtype),
        ),
        in_specs=[smem, tail(queries.shape[-1]), tail(2 * HEAD), hbm, hbm, hbm],
        out_specs=(hbm, hbm),
        input_output_aliases={4: 0, 5: 1},
        scratch_shapes=[
            pltpu.VMEM((entries, tiles * SPAN, CHUNK_ROWS, HEAD), jnp.bfloat16),
            pltpu.VMEM((entries, STEPS, queries.shape[-1]), jnp.bfloat16),
            pltpu.SemaphoreType.DMA((4, tiles)),
            pltpu.SemaphoreType.DMA((4, tiles)),
            pltpu.SemaphoreType.DMA((4, tiles)),
            pltpu.SemaphoreType.DMA((4,)),
        ],
        compiler_params=pltpu.CompilerParams(vmem_limit_bytes=VMEM),
        cost_estimate=pl.CostEstimate(flops=1 << 30, bytes_accessed=8 << 20, transcendentals=1 << 20),
        name="moved_slots" if first == MOVED_LEN else "kept_slots",
    )(table, queries, fresh, codes, out, arrived)


def leave_kernel(shift, table_ref, codes_ref, out_ref, hold, in_sem, out_sem):
    chunks = out_ref.shape[0]
    parts = [pl.ds(start, min(LEAVING, chunks - start)) for start in range(0, chunks, LEAVING)]
    group = table_ref[SEND + shift]

    def fetch(n):
        return pltpu.make_async_copy(codes_ref.at[group, parts[n]], hold.at[parts[n]], in_sem.at[n])

    def place(n):
        return pltpu.make_async_copy(hold.at[parts[n]], out_ref.at[parts[n]], out_sem.at[n])

    for n in range(len(parts)):
        fetch(n).start()
    for n in range(len(parts)):
        fetch(n).wait()
        place(n).start()
    for n in range(len(parts)):
        place(n).wait()


def leave(shift, size, table, codes):
    hbm = pl.BlockSpec(memory_space=pltpu.HBM)
    shape = (size // CHUNK,) + codes.shape[2:]
    copies = pl.cdiv(shape[0], LEAVING)
    return pl.pallas_call(
        functools.partial(leave_kernel, shift),
        out_shape=jax.ShapeDtypeStruct(shape, codes.dtype),
        in_specs=[pl.BlockSpec(memory_space=pltpu.SMEM), hbm],
        out_specs=hbm,
        scratch_shapes=[
            pltpu.VMEM(shape, codes.dtype),
            pltpu.SemaphoreType.DMA((copies,)),
            pltpu.SemaphoreType.DMA((copies,)),
        ],
        compiler_params=pltpu.CompilerParams(vmem_limit_bytes=VMEM),
        name="leave",
    )(table, codes)


def shifted(values, shift):
    return lax.ppermute(values, "src", [(g, (g + shift) % 4) for g in range(4)])


def on_device(
    prefill_pool,
    block_scales,
    block_table,
    prompt_len,
    dest_group,
    res_len,
    res_cache,
    queries,
    new_kv,
):
    everywhere = ("src", "section", "tp")
    me = lax.axis_index("src").astype(jnp.int32).reshape(1)
    layers, heads, block_len, width = prefill_pool.shape[4:]
    pool = prefill_pool.reshape(16, layers * heads, block_len, width)
    slots = queries.shape[1] - res_cache.shape[1]
    positions = 32 * 4 * block_len
    query_view, fresh_view = queries[0, :, 0], new_kv[0, :, 0]

    scales = block_scales.reshape(16, layers * heads, 2).transpose(1, 2, 0).reshape(layers * heads * 2, 16)
    dest = dest_group.transpose(0, 2, 1)
    packed, ready = pack(me, dest, prompt_len, block_table, scales, pool)
    landed = lax.all_to_all(
        packed.reshape(128, CHUNK_ROWS, HEAD), everywhere, split_axis=0, concat_axis=0, tiled=True
    ).reshape(4, 32, CHUNK_ROWS, HEAD)
    out, arrived, table = resident(
        ready, dest, prompt_len, res_len, query_view, fresh_view, res_cache[0, :, 0], slots, positions
    )

    def kept(landed, out, arrived):
        return fill_slots(KEPT_LEN, False, table, query_view, fresh_view, landed, out, arrived)

    def moved(shared, codes, out, arrived):
        return fill_slots(MOVED_LEN, shared, table, query_view, fresh_view, codes, out, arrived)

    def general(landed, out, arrived):
        codes = jnp.zeros_like(landed)
        for shift in range(1, 4):
            hit = table[MOVED_SHIFT : MOVED_SHIFT + 4] == shift
            codes = jnp.where(hit[:, None, None, None], shifted(landed, shift), codes)
        out, arrived = kept(landed, out, arrived)
        return moved(False, codes, out, arrived)

    def direct(shift, size, landed, out, arrived):
        codes = shifted(leave(shift, size, table, landed), shift)
        out, arrived = kept(landed, out, arrived)
        return moved(True, codes, out, arrived)

    branches = [general] + [
        functools.partial(direct, shift, size) for shift in range(1, 4) for size in SIZES
    ]
    out, arrived = lax.switch(table[BRANCH], branches, landed, out, arrived)
    return out[None, :, None], arrived.reshape(slots, positions, width)[None, :, None]


def solution(mesh):
    return jax.shard_map(
        on_device,
        mesh=mesh,
        in_specs=(
            P("src", "section", "tp", None, None, None, None, None),
            P("src", "section", "tp", None, None, None, None),
            P("src", "section", "tp", None),
            P(),
            P(),
            P("src", None),
            P("section", "src", "tp", None, None),
            P("section", "src", "tp", None, None),
            P("section", "src", "tp", None, None),
        ),
        out_specs=(P("section", "src", "tp", None, None), P("section", "src", "tp", None, None)),
        check_vma=False,
    )
```

```python
import functools
import math

import jax
import jax.numpy as jnp
from jax import lax
from jax.experimental import pallas as pl
from jax.experimental.pallas import tpu as pltpu
from jax.sharding import PartitionSpec as P

HEAD = 128
STEPS = 8
GROUP = 16
QUERIES = STEPS * GROUP
TILE = 512
BLOCK = 16
CHUNK = 4 * BLOCK
SPAN = TILE // CHUNK
FACTORS = 2 * CHUNK
CHUNK_ROWS = 2 * CHUNK + 8
LEAVING = 4
EXPONENT = math.log2(math.e) / math.sqrt(HEAD)
SIZES = (640, 896, 1280, 2048)
VMEM = 66_950_000

KEPT_LEN, KEPT_SLOT = 0, 4
MOVED_LEN, MOVED_SLOT, MOVED_SHIFT = 8, 12, 16
SEND, BRANCH = 20, 24
TABLE = 32


def routes(dest, length):
    count = len(dest)
    same = [[dest[i] == dest[j] for j in range(count)] for i in range(count)]
    one = lambda flag: jnp.where(flag, 1, 0)
    moved, rank = [], []
    for i in range(count):
        flag = jnp.int32(0)
        place = jnp.int32(0)
        for j in range(count):
            if j == i:
                continue
            longer = length[j] >= length[i] if j < i else length[j] > length[i]
            flag = flag + one(jnp.logical_and(same[i][j], longer))
            if j < i:
                place = place + one(same[i][j])
        moved.append(flag > 0)
        rank.append(place)
    free = []
    for plane in range(count):
        named = jnp.int32(0)
        for i in range(count):
            named = named + one(dest[i] == plane)
        free.append(named == 0)
    planes = []
    before = jnp.int32(0)
    for i in range(count):
        choice = jnp.int32(0)
        seen = jnp.int32(0)
        for plane in range(count):
            choice = jnp.where(jnp.logical_and(free[plane], seen == before), plane, choice)
            seen = seen + one(free[plane])
        planes.append(jnp.where(moved[i], choice, dest[i]))
        before = before + one(moved[i])
    return planes, moved, rank


def fill_table(me, dest_ref, len_ref, table_ref):
    groups, requests = 4, 4
    for n in range(TABLE):
        table_ref[n] = 0
    crowded = jnp.int32(0)
    longest = jnp.int32(0)
    shifts_used = [jnp.int32(0)] * 4
    at_plane = [[jnp.int32(0)] * 4 for _ in range(4)]
    for g in range(groups):
        dest = [dest_ref[g, 0, i] for i in range(requests)]
        length = [len_ref[g, i] for i in range(requests)]
        planes, moved, rank = routes(dest, length)
        for i in range(requests):
            slot = g * 2 + rank[i]
            shift = (dest[i] - planes[i] + 4) & 3
            kept = jnp.logical_and(dest[i] == me, jnp.logical_not(moved[i]))

            @pl.when(kept)
            def _():
                table_ref[KEPT_LEN + g] = length[i]
                table_ref[KEPT_SLOT + g] = slot

            @pl.when(jnp.logical_and(moved[i], dest[i] == me))
            def _():
                table_ref[MOVED_LEN + g] = length[i]
                table_ref[MOVED_SLOT + g] = slot
                table_ref[MOVED_SHIFT + g] = shift

            @pl.when(jnp.logical_and(moved[i], planes[i] == me))
            def _():
                table_ref[SEND + shift] = g

            longest = jnp.where(moved[i], jnp.maximum(longest, length[i]), longest)
            for s in range(1, 4):
                hit = jnp.logical_and(moved[i], shift == s)
                shifts_used[s] = jnp.where(hit, 1, shifts_used[s])
                for m in range(4):
                    more = at_plane[m][s] + jnp.where(jnp.logical_and(hit, planes[i] == m), 1, 0)
                    at_plane[m][s] = more
                    crowded = jnp.where(more > 1, 1, crowded)
    kinds = shifts_used[1] + shifts_used[2] + shifts_used[3]
    which = shifts_used[2] + 2 * shifts_used[3]
    size = jnp.int32(0)
    for limit in SIZES[:-1]:
        size = size + jnp.where(longest > limit, 1, 0)
    simple = jnp.logical_and(kinds == 1, crowded == 0)
    table_ref[BRANCH] = jnp.where(simple, 1 + which * len(SIZES) + size, 0)


def pack_kernel(
    me_ref, dest_ref, len_ref, block_ref, scale_ref, pool_ref, out_ref, ready_ref,
    hold, wide, in_sem, key_sem, value_sem, wide_sem,
):
    requests = 4
    me = me_ref[0]
    ready_ref[0] = me

    def fetch(n):
        rows = pl.ds((n % 4) * BLOCK, BLOCK)
        return pltpu.make_async_copy(pool_ref.at[block_ref[0, 0, 0, n]], hold.at[n // 4, :, rows], in_sem.at[n])

    for n in range(16):
        fetch(n).start()
    own_planes, _, _ = routes(
        [dest_ref[me, 0, i] for i in range(requests)],
        [len_ref[me, i] for i in range(requests)],
    )

    def place(i):
        rows = out_ref.at[own_planes[i]]
        keys = hold.at[i, :, :, pl.ds(0, HEAD)]
        values = hold.at[i, :, :, pl.ds(HEAD, HEAD)]
        return (
            pltpu.make_async_copy(keys, rows.at[:, pl.ds(0, CHUNK)], key_sem.at[i]),
            pltpu.make_async_copy(values, rows.at[:, pl.ds(CHUNK, CHUNK)], value_sem.at[i]),
        )

    def place_factors(i):
        rows = out_ref.at[own_planes[i], :, pl.ds(FACTORS, 8)]
        return pltpu.make_async_copy(wide.at[i], rows, wide_sem.at[i])

    pairs = scale_ref[...]
    row = lax.broadcasted_iota(jnp.int32, (4 * pairs.shape[0], pairs.shape[0]), 0)
    column = lax.broadcasted_iota(jnp.int32, row.shape, 1)
    repeat = jnp.where(column == (row >> 3) * 2 + (row & 1), 1.0, 0.0).astype(jnp.bfloat16)
    scales = jnp.dot(repeat, pairs, preferred_element_type=jnp.float32)
    block = (lax.broadcasted_iota(jnp.int32, scales.shape, 0) >> 1) & 3
    entry = lax.broadcasted_iota(jnp.int32, scales.shape, 1)
    ones = jnp.ones((scales.shape[1], HEAD), jnp.bfloat16)
    for i in range(requests):
        wanted = jnp.full(scales.shape, block_ref[0, 0, 0, 4 * i], jnp.int32)
        for k in range(1, 4):
            wanted = jnp.where(block == k, block_ref[0, 0, 0, 4 * i + k], wanted)
        picked = jnp.where(entry == wanted, scales, 0.0).astype(jnp.bfloat16)
        spread = jnp.dot(picked, ones, preferred_element_type=jnp.float32)
        wide[i] = spread.reshape(wide.shape[1:]).astype(jnp.bfloat16)
        place_factors(i).start()

    for i in range(requests):
        for k in range(4):
            fetch(4 * i + k).wait()
        for copy in place(i):
            copy.start()

    for i in range(requests):
        for copy in place(i):
            copy.wait()
        place_factors(i).wait()


def pack(me, dest, lengths, blocks, scales, pool):
    smem = pl.BlockSpec(memory_space=pltpu.SMEM)
    vmem = pl.BlockSpec(memory_space=pltpu.VMEM)
    hbm = pl.BlockSpec(memory_space=pltpu.HBM)
    return pl.pallas_call(
        pack_kernel,
        out_shape=(
            jax.ShapeDtypeStruct((4, 32, CHUNK_ROWS, HEAD), jnp.bfloat16),
            jax.ShapeDtypeStruct((1,), jnp.int32),
        ),
        in_specs=[smem, smem, smem, smem, vmem, hbm],
        out_specs=(hbm, smem),
        scratch_shapes=[
            pltpu.VMEM((4, 32, CHUNK, 2 * HEAD), jnp.bfloat16),
            pltpu.VMEM((4, 32, 8, HEAD), jnp.bfloat16),
            pltpu.SemaphoreType.DMA((16,)),
            pltpu.SemaphoreType.DMA((4,)),
            pltpu.SemaphoreType.DMA((4,)),
            pltpu.SemaphoreType.DMA((4,)),
        ],
        compiler_params=pltpu.CompilerParams(vmem_limit_bytes=VMEM),
        cost_estimate=pl.CostEstimate(flops=0, bytes_accessed=8 << 20, transcendentals=0),
        name="pack",
    )(me, dest, lengths, blocks, scales, pool)


def query_rows(query):
    wide = query.astype(jnp.float32)
    return jnp.concatenate([wide[:, q * HEAD : (q + 1) * HEAD] for q in range(GROUP)], axis=0).astype(
        jnp.bfloat16
    )


def against(rows, keys):
    return lax.dot_general(rows, keys, (((1,), (1,)), ((), ())), preferred_element_type=jnp.float32)


def open_row(rows, fresh):
    scores = against(rows, fresh[:, :HEAD])
    step = lax.broadcasted_iota(jnp.int32, scores.shape, 0) & (STEPS - 1)
    key = lax.broadcasted_iota(jnp.int32, scores.shape, 1)
    scores = jnp.where(key <= step, scores, -jnp.inf)
    top = jnp.max(scores, axis=1, keepdims=True)
    weights = jnp.exp2((scores - top) * EXPONENT)
    mass = jnp.sum(weights, axis=1, keepdims=True)
    total = jnp.dot(weights.astype(jnp.bfloat16), fresh[:, HEAD:], preferred_element_type=jnp.float32)
    return top, mass, total


def extend_row(state, rows, keys, values, left):
    top, mass, total = state
    scores = against(rows, keys)
    key = lax.broadcasted_iota(jnp.int32, scores.shape, 1)
    scores = jnp.where(key < left, scores, -jnp.inf)
    higher = jnp.maximum(top, jnp.max(scores, axis=1, keepdims=True))
    fade = jnp.exp2((top - higher) * EXPONENT)
    weights = jnp.exp2((scores - higher) * EXPONENT)
    mass = mass * fade + jnp.sum(weights, axis=1, keepdims=True)
    total = total * fade + jnp.dot(weights.astype(jnp.bfloat16), values, preferred_element_type=jnp.float32)
    return higher, mass, total


def close_row(state):
    _, mass, total = state
    done = total / mass
    return jnp.concatenate([done[q * STEPS : (q + 1) * STEPS] for q in range(GROUP)], axis=1).astype(
        jnp.bfloat16
    )


def resident_kernel(
    ready_ref, dest_ref, prompt_ref, len_ref, query_ref, fresh_ref, cache_ref, out_ref, arrived_ref, table_ref,
    hold, zeros, in_sem, zero_sem,
):
    resident, context = cache_ref.shape[0], cache_ref.shape[1]
    tiles = context // TILE
    slots = arrived_ref.shape[0]

    def fetch(r, c):
        part = pl.ds(c * TILE, TILE)
        return pltpu.make_async_copy(cache_ref.at[r, part], hold.at[r, part], in_sem.at[r, c])

    for r in range(resident):
        for c in range(tiles):

            @pl.when(c * TILE < len_ref[0, r])
            def _():
                fetch(r, c).start()

    def clear(s):
        return pltpu.make_async_copy(zeros, arrived_ref.at[s], zero_sem.at[s])

    zeros[...] = jnp.zeros_like(zeros)
    for s in range(slots):
        clear(s).start()
    fill_table(ready_ref[0], dest_ref, prompt_ref, table_ref)

    def one_row(r, carry):
        rows = query_rows(query_ref[r])
        length = jnp.where(r < resident, len_ref[0, jnp.minimum(r, resident - 1)], 0)

        def tile(c, state):
            fetch(r, c).wait()
            part = pl.ds(pl.multiple_of(c * TILE, TILE), TILE)
            keys = hold[r, part, :HEAD]
            values = hold[r, part, HEAD:]
            return extend_row(state, rows, keys, values, length - c * TILE)

        state = lax.fori_loop(0, (length + TILE - 1) // TILE, tile, open_row(rows, fresh_ref[r]))
        out_ref[r] = close_row(state)
        return carry

    lax.fori_loop(0, query_ref.shape[0], one_row, 0)
    for s in range(slots):
        clear(s).wait()


def resident(ready, dest, prompts, lengths, queries, fresh, cache, slots, positions):
    smem = pl.BlockSpec(memory_space=pltpu.SMEM)
    vmem = pl.BlockSpec(memory_space=pltpu.VMEM)
    hbm = pl.BlockSpec(memory_space=pltpu.HBM)
    rows, context = cache.shape[0], cache.shape[1]
    return pl.pallas_call(
        resident_kernel,
        out_shape=(
            jax.ShapeDtypeStruct(queries.shape, jnp.bfloat16),
            jax.ShapeDtypeStruct((slots, positions // CHUNK, CHUNK, 2 * HEAD), jnp.bfloat16),
            jax.ShapeDtypeStruct((TABLE,), jnp.int32),
        ),
        in_specs=[smem, smem, smem, smem, vmem, vmem, hbm],
        out_specs=(vmem, hbm, smem),
        scratch_shapes=[
            pltpu.VMEM((rows, context, 2 * HEAD), jnp.bfloat16),
            pltpu.VMEM((positions // CHUNK, CHUNK, 2 * HEAD), jnp.bfloat16),
            pltpu.SemaphoreType.DMA((rows, context // TILE)),
            pltpu.SemaphoreType.DMA((slots,)),
        ],
        compiler_params=pltpu.CompilerParams(vmem_limit_bytes=VMEM),
        cost_estimate=pl.CostEstimate(flops=1 << 31, bytes_accessed=20 << 20, transcendentals=4 << 20),
        name="resident",
    )(ready, dest, prompts, lengths, queries, fresh, cache)


def slot_kernel(
    first, shared, table_ref, query_ref, fresh_ref, codes_ref, _out, _arrived, out_ref, arrived_ref,
    hold, answer, in_sem, key_sem, value_sem, answer_sem,
):
    resident = out_ref.shape[0] - query_ref.shape[0]
    chunks = codes_ref.shape[-3]
    tiles = pl.cdiv(chunks, SPAN)
    groups = 4

    def fetch(g, c, count=None):
        part = pl.ds(c * SPAN, count or min(SPAN, chunks - c * SPAN))
        if shared:
            return pltpu.make_async_copy(codes_ref.at[part], hold.at[0, part], in_sem.at[g, c])
        return pltpu.make_async_copy(codes_ref.at[g, part], hold.at[g, part], in_sem.at[g, c])

    def put(g, c):
        part = pl.ds(c * SPAN, SPAN)
        slot = table_ref[first + 4 + g]
        chunks = hold.at[0 if shared else g, part]
        target = arrived_ref.at[slot, part]
        return (
            pltpu.make_async_copy(chunks.at[:, pl.ds(0, CHUNK)], target.at[:, :, pl.ds(0, HEAD)], key_sem.at[g, c]),
            pltpu.make_async_copy(
                chunks.at[:, pl.ds(CHUNK, CHUNK)], target.at[:, :, pl.ds(HEAD, HEAD)], value_sem.at[g, c]
            ),
        )

    def reply(g):
        slot = table_ref[first + 4 + g]
        return pltpu.make_async_copy(answer.at[0 if shared else g], out_ref.at[resident + slot], answer_sem.at[g])

    def inside(codes, left):
        chunk = lax.broadcasted_iota(jnp.int32, codes.shape, 0)
        row = lax.broadcasted_iota(jnp.int32, codes.shape, 1) & (CHUNK - 1)
        return jnp.where(chunk * CHUNK + row < left, codes.astype(jnp.float32), 0.0).astype(jnp.bfloat16)

    if chunks < tiles * SPAN:
        rest = pl.ds(chunks, tiles * SPAN - chunks)
        hold[0, rest, :, :] = jnp.zeros_like(hold[0, rest, :, :])
    for g in range(groups):
        for c in range(tiles):

            @pl.when(c * TILE < table_ref[first + g])
            def _():
                fetch(g, c).start()

    def scaled(codes, factors, which):
        wide = codes.astype(jnp.float32)
        rows = []
        for p in range(SPAN):
            for k in range(CHUNK // BLOCK):
                factor = factors[p, 2 * k + which : 2 * k + which + 1, :]
                rows.append(wide[p, k * BLOCK : (k + 1) * BLOCK, :] * factor)
        return jnp.concatenate(rows, axis=0).astype(jnp.bfloat16)

    def one_slot(g, carry):
        length = table_ref[first + g]
        slot = table_ref[first + 4 + g]
        at = 0 if shared else g

        @pl.when(length > 0)
        def _():
            rows = query_rows(query_ref[slot])

            def tile(c, state):
                part = pl.ds(pl.multiple_of(c * SPAN, SPAN), SPAN)
                left = length - c * TILE
                if chunks == tiles * SPAN:
                    fetch(g, c, SPAN).wait()
                else:

                    @pl.when(c < tiles - 1)
                    def _():
                        fetch(g, c, SPAN).wait()

                    @pl.when(c == tiles - 1)
                    def _():
                        fetch(g, tiles - 1).wait()

                @pl.when(left < TILE)
                def _():
                    hold[at, part, :FACTORS, :] = inside(hold[at, part, :FACTORS, :], left)

                factors = hold[at, part, FACTORS:, :].astype(jnp.float32)
                for copy in put(g, c):
                    copy.start()
                keys = scaled(hold[at, part, :CHUNK, :], factors, 0)
                values = scaled(hold[at, part, CHUNK:FACTORS, :], factors, 1)
                return extend_row(state, rows, keys, values, left)

            state = lax.fori_loop(0, (length + TILE - 1) // TILE, tile, open_row(rows, fresh_ref[slot]))
            answer[at] = close_row(state)
            reply(g).start()

        return carry

    lax.fori_loop(0, groups, one_slot, 0)
    for g in range(groups):

        @pl.when(table_ref[first + g] > 0)
        def _():
            reply(g).wait()

        for c in range(tiles):

            @pl.when(c * TILE < table_ref[first + g])
            def _():
                for copy in put(g, c):
                    copy.wait()


def fill_slots(first, shared, table, queries, fresh, codes, out, arrived):
    smem = pl.BlockSpec(memory_space=pltpu.SMEM)
    vmem = pl.BlockSpec(memory_space=pltpu.VMEM)
    hbm = pl.BlockSpec(memory_space=pltpu.HBM)
    slots = arrived.shape[0]
    entries, tiles = 1 if shared else codes.shape[0], pl.cdiv(codes.shape[-3], SPAN)
    tail = lambda width: pl.BlockSpec((slots, STEPS, width), lambda n: (1, 0, 0))
    return pl.pallas_call(
        functools.partial(slot_kernel, first, shared),
        grid=(1,),
        out_shape=(
            jax.ShapeDtypeStruct(out.shape, out.dtype),
            jax.ShapeDtypeStruct(arrived.shape, arrived.dtype),
        ),
        in_specs=[smem, tail(queries.shape[-1]), tail(2 * HEAD), hbm, hbm, hbm],
        out_specs=(hbm, hbm),
        input_output_aliases={4: 0, 5: 1},
        scratch_shapes=[
            pltpu.VMEM((entries, tiles * SPAN, CHUNK_ROWS, HEAD), jnp.bfloat16),
            pltpu.VMEM((entries, STEPS, queries.shape[-1]), jnp.bfloat16),
            pltpu.SemaphoreType.DMA((4, tiles)),
            pltpu.SemaphoreType.DMA((4, tiles)),
            pltpu.SemaphoreType.DMA((4, tiles)),
            pltpu.SemaphoreType.DMA((4,)),
        ],
        compiler_params=pltpu.CompilerParams(vmem_limit_bytes=VMEM),
        cost_estimate=pl.CostEstimate(flops=1 << 30, bytes_accessed=8 << 20, transcendentals=1 << 20),
        name="moved_slots" if first == MOVED_LEN else "kept_slots",
    )(table, queries, fresh, codes, out, arrived)


def leave_kernel(shift, table_ref, codes_ref, out_ref, hold, in_sem, out_sem):
    chunks = out_ref.shape[0]
    parts = [pl.ds(start, min(LEAVING, chunks - start)) for start in range(0, chunks, LEAVING)]
    group = table_ref[SEND + shift]

    def fetch(n):
        return pltpu.make_async_copy(codes_ref.at[group, parts[n]], hold.at[parts[n]], in_sem.at[n])

    def place(n):
        return pltpu.make_async_copy(hold.at[parts[n]], out_ref.at[parts[n]], out_sem.at[n])

    for n in range(len(parts)):
        fetch(n).start()
    for n in range(len(parts)):
        fetch(n).wait()
        place(n).start()
    for n in range(len(parts)):
        place(n).wait()


def leave(shift, size, table, codes):
    hbm = pl.BlockSpec(memory_space=pltpu.HBM)
    shape = (size // CHUNK,) + codes.shape[2:]
    copies = pl.cdiv(shape[0], LEAVING)
    return pl.pallas_call(
        functools.partial(leave_kernel, shift),
        out_shape=jax.ShapeDtypeStruct(shape, codes.dtype),
        in_specs=[pl.BlockSpec(memory_space=pltpu.SMEM), hbm],
        out_specs=hbm,
        scratch_shapes=[
            pltpu.VMEM(shape, codes.dtype),
            pltpu.SemaphoreType.DMA((copies,)),
            pltpu.SemaphoreType.DMA((copies,)),
        ],
        compiler_params=pltpu.CompilerParams(vmem_limit_bytes=VMEM),
        name="leave",
    )(table, codes)


def shifted(values, shift):
    return lax.ppermute(values, "src", [(g, (g + shift) % 4) for g in range(4)])


def on_device(
    prefill_pool,
    block_scales,
    block_table,
    prompt_len,
    dest_group,
    res_len,
    res_cache,
    queries,
    new_kv,
):
    everywhere = ("src", "section", "tp")
    me = lax.axis_index("src").astype(jnp.int32).reshape(1)
    layers, heads, block_len, width = prefill_pool.shape[4:]
    pool = prefill_pool.reshape(16, layers * heads, block_len, width)
    slots = queries.shape[1] - res_cache.shape[1]
    positions = 32 * 4 * block_len
    query_view, fresh_view = queries[0, :, 0], new_kv[0, :, 0]

    scales = block_scales.reshape(16, layers * heads, 2).transpose(1, 2, 0).reshape(layers * heads * 2, 16)
    dest = dest_group.transpose(0, 2, 1)
    packed, ready = pack(me, dest, prompt_len, block_table, scales, pool)
    landed = lax.all_to_all(
        packed.reshape(128, CHUNK_ROWS, HEAD), everywhere, split_axis=0, concat_axis=0, tiled=True
    ).reshape(4, 32, CHUNK_ROWS, HEAD)
    out, arrived, table = resident(
        ready, dest, prompt_len, res_len, query_view, fresh_view, res_cache[0, :, 0], slots, positions
    )

    def kept(landed, out, arrived):
        return fill_slots(KEPT_LEN, False, table, query_view, fresh_view, landed, out, arrived)

    def moved(shared, codes, out, arrived):
        return fill_slots(MOVED_LEN, shared, table, query_view, fresh_view, codes, out, arrived)

    def general(landed, out, arrived):
        codes = jnp.zeros_like(landed)
        for shift in range(1, 4):
            hit = table[MOVED_SHIFT : MOVED_SHIFT + 4] == shift
            codes = jnp.where(hit[:, None, None, None], shifted(landed, shift), codes)
        out, arrived = kept(landed, out, arrived)
        return moved(False, codes, out, arrived)

    def direct(shift, size, landed, out, arrived):
        codes = shifted(leave(shift, size, table, landed), shift)
        out, arrived = kept(landed, out, arrived)
        return moved(True, codes, out, arrived)

    branches = [general] + [
        functools.partial(direct, shift, size) for shift in range(1, 4) for size in SIZES
    ]
    out, arrived = lax.switch(table[BRANCH], branches, landed, out, arrived)
    return out[None, :, None], arrived.reshape(slots, positions, width)[None, :, None]


def solution(mesh):
    return jax.shard_map(
        on_device,
        mesh=mesh,
        in_specs=(
            P("src", "section", "tp", None, None, None, None, None),
            P("src", "section", "tp", None, None, None, None),
            P("src", "section", "tp", None),
            P(),
            P(),
            P("src", None),
            P("section", "src", "tp", None, None),
            P("section", "src", "tp", None, None),
            P("section", "src", "tp", None, None),
        ),
        out_specs=(P("section", "src", "tp", None, None), P("section", "src", "tp", None, None)),
        check_vma=False,
    )
```
